256 devices in a mesh: vtx: 64 (over y_hi, z, x), feat: 4 (over y_lo, core).
Axes of the slice: x: 4, y: 4 (y_hi: 2, y_lo: 2; y = y_hi * 2 + y_lo), z: 8, core: 2. Of those that a mesh axis runs over, the one named last changes fastest.
Arguments:
- features: bfloat16 [16384, 128], P('vtx'), may hold values from -6 to 6
- weight: bfloat16 [128, 512], P(None, 'feat'), may hold values from -0.5 to 0.5
- bias: float32 [512], P('feat'), may hold values from -3 to 3
- cotangent: bfloat16 [16384, 512], P('vtx', 'feat'), may hold values from -6 to 6
- adj_tiles: bfloat16 [16384, 128, 128], P('vtx'), may hold values from 0 to 0.039794922
- tile_rows: int32 [4096, 4], P('vtx'), may hold values from 0 to 1
- tile_cols: int32 [4096, 4], P('vtx'), may hold values from 0 to 1
- tile_counts: int32 [4096], P('vtx'), may hold values from 0 to 4, as said below
Outputs:
- output: bfloat16 [16384, 512], P('vtx', 'feat')
- grad_features: bfloat16 [16384, 128], P('vtx', 'feat')
- grad_weight: float32 [128, 512], P(None, 'feat')
- grad_bias: float32 [512], P('feat')
The draws below stay inside these ranges and needn't reach their ends.
Inputs may be any that keep to these rules, and one draw needn't show every extreme that they name: `tile_counts`: A pair's count is at most 4; every diagonal pair d * 64 + d holds exactly 4; counts are skewed over row blocks.
All inputs are finite; a program needn't handle non-finite values.
Results may differ from the reference program's by a relative error of at most 0.007.
Values may be sent and summed in bfloat16 or wider, within the bound.
A program may use at most 128 MiB of HBM per device.

```python
import jax
import jax.numpy as jnp
from jax import lax

ROWS_DEV = 256
TILE = 128
SLOTS = 4
FEATS = 128
HIDDEN_SIZE = 512
BLOCKS = 64
NODES = 16384
PAIRS = 4096
ALL_SLOTS = 16384


def draw_tile_counts(key, part):
    key = jax.random.fold_in(key, 7)
    key_heavy, key_light, key_busy = jax.random.split(key, 3)
    heavy = jax.random.randint(key_heavy, (BLOCKS, 1), 0, 4) == 0
    light_count = jax.random.randint(key_light, (BLOCKS, BLOCKS), 0, 2)
    busy_count = jax.random.randint(key_busy, (BLOCKS, BLOCKS), 1, SLOTS + 1)
    counts = jnp.where(heavy, busy_count, light_count)
    diagonal = jnp.eye(BLOCKS, dtype=bool)
    counts = jnp.where(diagonal, SLOTS, counts)
    return counts.reshape(BLOCKS * BLOCKS).astype(jnp.int32)


def with_ends(array, own_key, smallest, top_value):
    longest = array.shape.index(max(array.shape))
    spots = []
    for shift in (0, 1):
        where = [jax.random.randint(jax.random.fold_in(own_key, axis), (), 0, length) for axis, length in enumerate(array.shape)]
        where[longest] = (where[longest] + shift) % array.shape[longest]
        spots.append(tuple(where))
    return array.at[spots[0]].set(smallest).at[spots[1]].set(top_value)


def block_levels(stream_key, dims, cuts, least, high):
    level, own = 1.0, jax.random.fold_in(stream_key, 6)
    for dim, shards_of in cuts:
        heights = jnp.exp(jax.random.uniform(jax.random.fold_in(own, dim), (shards_of,), jnp.float32, least / len(cuts), high / len(cuts)))
        level = level * jnp.repeat(heights, dims[dim] // shards_of).reshape([-1 if axis == dim else 1 for axis in range(len(dims))])
    return level


def gaussian(rng, shape, width, bound, pieces=(), kind=jnp.bfloat16):
    gain = block_levels(rng, shape, pieces, -0.22, 0.18) if pieces else 1.0
    array = jax.random.normal(rng, shape, jnp.float32) * width * gain
    return jnp.minimum(jnp.maximum(array, -bound), bound).astype(kind)


def setup_inputs(seed: int = 0) -> dict:
    keys = jax.random.split(jax.random.key(seed), 9)
    return {
        "features": gaussian(keys[0], (NODES, FEATS), 1.0, 6.0, ((0, 64),)),
        "weight": gaussian(keys[1], (FEATS, HIDDEN_SIZE), FEATS ** -0.5, 0.5, ((1, 4),)),
        "bias": gaussian(keys[2], (HIDDEN_SIZE,), 0.5, 3.0, ((0, 4),), jnp.float32),
        "cotangent": gaussian(keys[3], (NODES, HIDDEN_SIZE), 1.0, 6.0, ((0, 64), (1, 4))),
        "adj_tiles": jnp.clip(0.039794922 * jax.random.uniform(keys[4], (ALL_SLOTS, TILE, TILE), jnp.float32) ** block_levels(keys[4], (ALL_SLOTS, TILE, TILE), ((0, 64),), -0.2, 0.2), 0.0, 0.039794922).astype(jnp.bfloat16),
        "tile_rows": with_ends(jax.random.randint(keys[5], (PAIRS, SLOTS), 0, ROWS_DEV // TILE), jax.random.fold_in(keys[5], 1), 0, (ROWS_DEV // TILE) - 1).astype(jnp.int32),
        "tile_cols": with_ends(jax.random.randint(keys[6], (PAIRS, SLOTS), 0, ROWS_DEV // TILE), jax.random.fold_in(keys[6], 1), 0, (ROWS_DEV // TILE) - 1).astype(jnp.int32),
        "tile_counts": draw_tile_counts(jax.random.fold_in(keys[8], 71), 0),
    }


def activation(v):
    return jax.nn.gelu(v, approximate=True)

def reference(features, weight, bias, cotangent, adj_tiles, tile_rows, tile_cols, tile_counts):
    row_tiles = ROWS_DEV // TILE
    highest = lax.Precision.HIGHEST
    hidden = jnp.dot(features, weight, preferred_element_type=jnp.float32).astype(jnp.bfloat16)
    hid_tiles = hidden.reshape(BLOCKS * row_tiles, TILE, HIDDEN_SIZE)
    tiles_five = adj_tiles.reshape(BLOCKS, BLOCKS, SLOTS, TILE, TILE)
    rows_three = tile_rows.reshape(BLOCKS, BLOCKS, SLOTS).astype(jnp.int32)
    cols_three = tile_cols.reshape(BLOCKS, BLOCKS, SLOTS).astype(jnp.int32)
    counts_two = tile_counts.reshape(BLOCKS, BLOCKS).astype(jnp.int32)
    base = (jnp.arange(BLOCKS, dtype=jnp.int32) * row_tiles)[:, None]
    slot_ids = jnp.arange(SLOTS, dtype=jnp.int32)
    tile_ids = jnp.arange(row_tiles, dtype=jnp.int32)
    valid = (slot_ids[None, None, :] < counts_two[:, :, None]).astype(jnp.float32)

    def forward_rows(block):
        source = hid_tiles[base + cols_three[block]]
        prod = jnp.einsum('skij,skjc->skic', tiles_five[block].astype(jnp.float32), source.astype(jnp.float32), precision=highest)
        onehot = (rows_three[block][..., None] == tile_ids[None, None, :]).astype(jnp.float32) * valid[block][..., None]
        return jnp.einsum('skr,skic->ric', onehot, prod, precision=highest)
    aggregate = lax.map(forward_rows, jnp.arange(BLOCKS, dtype=jnp.int32)).reshape(NODES, HIDDEN_SIZE)
    pre = aggregate + bias
    result, pullback = jax.vjp(activation, pre)
    output = result.astype(jnp.bfloat16)
    grad_pre = pullback(cotangent.astype(jnp.float32))[0].astype(jnp.bfloat16)
    grad_tiles = grad_pre.reshape(BLOCKS, row_tiles, TILE, HIDDEN_SIZE)

    def backward_rows(total, block):
        source = grad_tiles[block][rows_three[block]]
        prod = jnp.einsum('skji,skjc->skic', tiles_five[block].astype(jnp.float32), source.astype(jnp.float32), precision=highest)
        prod = prod * valid[block][..., None, None]
        target = (base + cols_three[block]).reshape(-1)
        return (total.at[target].add(prod.reshape(-1, TILE, HIDDEN_SIZE)), None)
    start = jnp.zeros((BLOCKS * row_tiles, TILE, HIDDEN_SIZE), jnp.float32)
    grad_hidden, unused = lax.scan(backward_rows, start, jnp.arange(BLOCKS, dtype=jnp.int32))
    grad_round = grad_hidden.reshape(NODES, HIDDEN_SIZE).astype(jnp.bfloat16)
    grad_weight = jnp.dot(features.T, grad_round, preferred_element_type=jnp.float32)
    grad_bias = lax.optimization_barrier(jnp.sum(grad_pre.astype(jnp.float32), axis=0))
    grad_features = jnp.dot(grad_round, weight.T, preferred_element_type=jnp.float32).astype(jnp.bfloat16)
    return (output, grad_features, grad_weight, grad_bias)
```

```python
import functools
import math

import jax
import jax.numpy as jnp
from jax import lax
from jax.experimental import pallas as pl
from jax.experimental.pallas import tpu as pltpu
from jax.sharding import PartitionSpec as P

MESH = pl.DeviceIdType.MESH
RING_X = 4
T = 128
SLOTS = 4
F32 = jnp.float32
BF16 = jnp.bfloat16


def dot(a, b, dims=((1,), (0,))):
    return lax.dot_general(a, b, (dims, ((), ())), preferred_element_type=F32)


def split(v):
    high = v.astype(BF16)
    return high, (v - high.astype(F32)).astype(BF16)


def gelu_parts(v):
    c = math.sqrt(2.0 / math.pi)
    t = jnp.tanh(c * (v + 0.044715 * (v * v * v)))
    cdf = 0.5 * (1.0 + t)
    slope = cdf + 0.5 * v * (1.0 - t * t) * (c * (1.0 + (3.0 * 0.044715) * (v * v)))
    return v * cdf, slope


def kernel(
    Z,
    feat_h,
    weight_h,
    bias_h,
    cot_h,
    tiles_h,
    rows,
    cols,
    counts,
    out_ref,
    gf_ref,
    gw_ref,
    gb_ref,
    xg,
    tiles,
    w,
    bias,
    cot,
    acc,
    ex,
    sb,
    axf,
    gp,
    pt,
    pe,
    pb,
    pf,
    gwb,
    g1,
    g2s,
    g2,
    g3,
    sbuf,
    rbuf,
    fs,
    fr,
    lsem,
    ssem,
    rsem,
    exs,
    exr,
    gsem,
    g1r,
    g2r,
    g3r,
    tsem,
    trsem,
    fsem,
    frsem,
):
    X = RING_X
    H = Z // 2
    R = T // Z
    me_v = lax.axis_index("vtx")
    me_f = lax.axis_index("feat")
    h = me_v // (Z * X)
    z = (me_v // X) % Z
    x = me_v % X
    l = me_f // 2
    c = me_f % 2

    def vid(hh, zz, xx):
        return (hh * Z + zz) * X + xx

    def here(zz, xx):
        return (vid(h, zz, xx), me_f)

    core_mate = (me_v, l * 2 + 1 - c)
    lo_mate = (me_v, (1 - l) * 2 + c)
    swap_mate = (vid(1 - h, z, x), (1 - l) * 2 + c)

    def zat(o):
        return (z + Z + o) % Z

    def xat(o):
        return (x + X + o) % X

    def sgn(i):
        return 1 - 2 * (i % 2)

    def off(q):
        return ((q + 1) // 2) * (1 - 2 * (q % 2))

    p0 = z * X + x

    half_rows = pl.ds(pl.multiple_of(c * T, T), T)
    n_half = Z * X
    tiles_copy = pltpu.make_async_copy(
        tiles_h.at[pl.ds(l * (n_half * SLOTS), n_half * SLOTS)], tiles, lsem.at[0]
    )
    w_copy = pltpu.make_async_copy(weight_h, w, lsem.at[1])
    bias_copy = pltpu.make_async_copy(bias_h, bias, lsem.at[2])
    cot_copy = pltpu.make_async_copy(cot_h, cot, lsem.at[3])
    own_copy = pltpu.make_async_copy(feat_h.at[half_rows], xg.at[p0], lsem.at[4])

    @pl.when(h == l)
    def _():
        own_copy.start()

    tiles_copy.start()
    w_copy.start()
    bias_copy.start()
    cot_copy.start()

    barrier = pltpu.get_barrier_semaphore()

    def greet(v, f):
        pl.semaphore_signal(barrier, inc=1, device_id=(v, f), device_id_type=MESH)

    for dz in range(1, Z):
        greet(vid(h, zat(dz), x), me_f)
    for dx in range(1, X):
        greet(vid(h, z, xat(dx)), me_f)
    for dx in range(X):
        greet(vid(1 - h, z, xat(dx)), me_f)
    greet(*core_mate)
    greet(*lo_mate)
    greet(*swap_mate)
    acc[...] = jnp.zeros_like(acc)
    pl.semaphore_wait(barrier, (Z - 1) + (X - 1) + X + 3)

    def slot_copy(p, target):
        return pltpu.make_async_remote_copy(
            src_ref=xg.at[p],
            dst_ref=xg.at[p],
            send_sem=ssem.at[0],
            recv_sem=rsem.at[p],
            device_id=target,
            device_id_type=MESH,
        )

    def wait_slot(p):
        slot_copy(p, core_mate).wait_recv()

    swap_copy = pltpu.make_async_remote_copy(
        src_ref=feat_h.at[half_rows],
        dst_ref=xg.at[p0],
        send_sem=ssem.at[1],
        recv_sem=rsem.at[p0],
        device_id=swap_mate,
        device_id_type=MESH,
    )

    @pl.when(h != l)
    def _():
        swap_copy.start()
        swap_copy.wait()

    @pl.when(h == l)
    def _():
        own_copy.wait()

    def forward(p):
        s = l * n_half + p
        count = counts[s]
        block = xg[p]
        zero = jnp.zeros_like(block)
        right = []
        for k in range(SLOTS):
            ok = jnp.logical_and(k < count, cols[k, s] == c)
            r = rows[k, s]
            right.append(
                jnp.concatenate(
                    [
                        jnp.where(jnp.logical_and(ok, r == 0), block, zero),
                        jnp.where(jnp.logical_and(ok, r == 1), block, zero),
                    ],
                    axis=1,
                )
            )
        left = jnp.concatenate([tiles[p * SLOTS + k] for k in range(SLOTS)], axis=1)
        got = dot(left, jnp.concatenate(right, axis=0))
        acc[0] += got[:, :T]
        acc[1] += got[:, T:]

    def pass_z(q, col, p):
        hop = (q + 1) // 2
        sign = sgn(col)

        @pl.when(jnp.logical_and(q % 2 == 1, jnp.logical_or(hop < H - 1, jnp.logical_and(hop == H - 1, sign == 1))))
        def _():
            slot_copy(p, here(zat(1), x)).start()

        @pl.when(jnp.logical_and(q % 2 == 0, jnp.logical_or(hop < H - 1, jnp.logical_and(hop == H - 1, sign == -1))))
        def _():
            slot_copy(p, here(zat(-1), x)).start()

    def begin_z(col, p):
        if H > 1:
            slot_copy(p, here(zat(1), x)).start()
            slot_copy(p, here(zat(-1), x)).start()
        else:
            slot_copy(p, here(zat(1), x)).start()

    @pl.when(c == 0)
    def _():
        for dx in (1, 3, 2):
            slot_copy(p0, here(z, xat(dx))).start()
        begin_z(x, p0)
        tiles_copy.wait()
        forward(p0)

        def from_x(j, carry):
            col = xat(j + 1)
            p = z * X + col
            wait_slot(p)
            begin_z(col, p)
            forward(p)
            return carry

        lax.fori_loop(0, X - 1, from_x, 0)

        def from_z(t, carry):
            q = t // X + 1
            col = xat(t % X)
            p = zat(off(q)) * X + col
            wait_slot(p)
            pass_z(q, col, p)
            forward(p)
            return carry

        lax.fori_loop(0, (Z - 1) * X, from_z, 0)

    @pl.when(c == 1)
    def _():
        begin_z(x, p0)

        def begin_x(p):
            slot_copy(p, here(z, xat(1))).start()
            slot_copy(p, here(z, xat(3))).start()

        begin_x(p0)
        tiles_copy.wait()
        forward(p0)

        def row_x(zz):
            sign = sgn(zz)
            pm = zz * X + xat(-sign)
            pn = zz * X + xat(sign)
            wait_slot(pm)
            slot_copy(pm, here(z, xat(sign))).start()
            forward(pm)
            wait_slot(pn)
            forward(pn)

        def from_z(t, carry):
            q = t + 1
            p = zat(off(q)) * X + x
            wait_slot(p)
            pass_z(q, x, p)
            begin_x(p)
            forward(p)
            row_x(zat(off(q - 1)))
            return carry

        lax.fori_loop(0, Z - 1, from_z, 0)
        row_x(zat(off(Z - 1)))

        def from_far(q, carry):
            p = zat(off(q)) * X + xat(2)
            wait_slot(p)
            forward(p)
            return carry

        lax.fori_loop(0, Z, from_far, 0)

    def exchange(src, dst, i, target):
        return pltpu.make_async_remote_copy(
            src_ref=src,
            dst_ref=dst,
            send_sem=exs.at[i],
            recv_sem=exr.at[i],
            device_id=target,
            device_id_type=MESH,
        )

    first = exchange(acc.at[1 - c], ex.at[0], 0, core_mate)
    first.start()
    first.wait_recv()
    sb[...] = acc[c] + ex[0]
    second = exchange(sb, ex.at[1], 1, lo_mate)
    second.start()
    w_copy.wait()
    bias_copy.wait()
    cot_copy.wait()
    second.wait_recv()
    axf[c] = sb[...] + ex[1]
    third = exchange(axf.at[c], axf.at[c], 2, core_mate)
    third.start()

    def rows_half(r):
        high, low = split(axf[r])
        pre = dot(high, w[...]) + dot(low, w[...]) + bias[...]
        result, slope = gelu_parts(pre)
        where = pl.ds(pl.multiple_of(r * T, T), T)
        out_ref[where, :] = result.astype(BF16)
        grad = (cot[where, :].astype(F32) * slope).astype(BF16)
        gp[r] = grad
        back = dot(w[...], grad, ((1,), (1,)))
        for cc in range(2):
            for ll in range(2):
                pt[cc, r, ll * 32 : ll * 32 + 32, :] = back[ll * 64 + cc * 32 : ll * 64 + cc * 32 + 32, :]

    rows_half(c)
    exchange(axf.at[c], axf.at[1 - c], 2, core_mate).wait_recv()
    rows_half(1 - c)

    p_first = exchange(pt.at[1 - c], pe.at[0], 3, core_mate)
    p_first.start()

    local_w = jnp.zeros((T, T), F32)
    local_b = jnp.zeros((1, T), F32)
    for r in range(2):
        high, low = split(axf[r])
        grad = gp[r]
        local_w += dot(high, grad, ((0,), (0,))) + dot(low, grad, ((0,), (0,)))
        local_b += jnp.sum(grad.astype(F32), axis=0, keepdims=True)
    spread_b = jnp.broadcast_to(local_b, (8, T))
    for i in range(Z):
        gwb[i, :R, :] = local_w[i * R : i * R + R, :]
        gwb[i, R:, :] = spread_b

    def g1_copy(dz):
        return pltpu.make_async_remote_copy(
            src_ref=gwb.at[zat(dz)],
            dst_ref=g1.at[z],
            send_sem=gsem.at[0],
            recv_sem=g1r.at[z],
            device_id=here(zat(dz), x),
            device_id_type=MESH,
        )

    for dz in range(1, Z):
        g1_copy(dz).start()

    p_first.wait_recv()
    pb[...] = pt[c] + pe[0]
    p_second = exchange(pb, pe.at[1], 4, lo_mate)
    p_second.start()
    p_second.wait_recv()
    pf[...] = (pb[...] + pe[1]).astype(BF16)

    def own(p):
        s = l * n_half + p
        count = counts[s]
        low = pf[0]
        high = pf[1]
        zero = jnp.zeros_like(low)
        left = []
        for k in range(SLOTS):
            ok = k < count
            col = cols[k, s]
            picked = jnp.where(rows[k, s] == 0, low, high)
            left.append(
                jnp.concatenate(
                    [
                        jnp.where(jnp.logical_and(ok, col == 0), picked, zero),
                        jnp.where(jnp.logical_and(ok, col == 1), picked, zero),
                    ],
                    axis=0,
                )
            )
        right = tiles[pl.ds(p * SLOTS, SLOTS)].reshape(SLOTS * T, T)
        return dot(jnp.concatenate(left, axis=1), right)

    def sum_copy(i, target):
        return pltpu.make_async_remote_copy(
            src_ref=sbuf.at[i],
            dst_ref=rbuf.at[i],
            send_sem=tsem.at[0],
            recv_sem=trsem.at[i],
            device_id=target,
            device_id_type=MESH,
        )

    def take(i):
        sum_copy(i, core_mate).wait_recv()
        return rbuf[i].astype(F32)

    def put(i, value, target):
        sbuf[i] = value.astype(BF16)
        sum_copy(i, target).start()

    last = Z - 1

    def z_direction(q, col):
        return jnp.where(q == last, sgn(col), 2 * (q % 2) - 1)

    def has_incoming(q, col):
        by_parity = (2 * (q % 2) - 1) == sgn(col)
        return jnp.logical_or(q + 2 < last, jnp.logical_and(q < last, jnp.logical_and(q + 2 >= last, by_parity)))

    def source_q(q):
        return jnp.minimum(q + 2, last)

    def weight_sums_one():
        total = gwb[z]
        for dz in range(1, Z):
            src = zat(dz)
            pltpu.make_async_remote_copy(
                src_ref=gwb.at[src],
                dst_ref=g1.at[src],
                send_sem=gsem.at[0],
                recv_sem=g1r.at[src],
                device_id=here(zat(dz), x),
                device_id_type=MESH,
            ).wait_recv()
            total = total + g1[src]
        g2s[...] = total
        for e in range(1, 2 * X):
            hh = (h + e // X) % 2
            xx = xat(e % X)
            pltpu.make_async_remote_copy(
                src_ref=g2s,
                dst_ref=g2.at[h * X + x],
                send_sem=gsem.at[1],
                recv_sem=g2r.at[h * X + x],
                device_id=(vid(hh, z, xx), me_f),
                device_id_type=MESH,
            ).start()

    def weight_sums_two():
        total = g2s[...]
        for e in range(1, 2 * X):
            hh = (h + e // X) % 2
            xx = xat(e % X)
            src = hh * X + xx
            pltpu.make_async_remote_copy(
                src_ref=g2s,
                dst_ref=g2.at[src],
                send_sem=gsem.at[1],
                recv_sem=g2r.at[src],
                device_id=(vid(hh, z, xx), me_f),
                device_id_type=MESH,
            ).wait_recv()
            total = total + g2[src]
        g3[z] = total[:R, :]
        gb_ref[...] = total[R : R + 1, :]
        for dz in range(1, Z):
            pltpu.make_async_remote_copy(
                src_ref=g3.at[z],
                dst_ref=g3.at[z],
                send_sem=gsem.at[2],
                recv_sem=g3r.at[z],
                device_id=here(zat(dz), x),
                device_id_type=MESH,
            ).start()

    def finish(total):
        for lp in range(2):
            for ct in range(2):
                fs[lp, ct] = total[ct * 64 + lp * 32 : ct * 64 + lp * 32 + 32, :]

    ZB = Z * X - X

    @pl.when(c == 0)
    def _():
        def along_z(t, carry):
            q = last - t // X
            col = xat(t % X + 1)
            value = own(((z + Z - off(q)) % Z) * X + col)
            i = (q - 1) * X + col
            d = z_direction(q, col)
            target = here((z + Z + d) % Z, x)

            @pl.when(has_incoming(q, col))
            def _():
                put(i, value + take((source_q(q) - 1) * X + col), target)

            @pl.when(jnp.logical_not(has_incoming(q, col)))
            def _():
                put(i, value, target)

            return carry

        half = (Z - 1) * X // 2
        lax.fori_loop(0, half, along_z, 0)
        weight_sums_one()
        lax.fori_loop(half, (Z - 1) * X, along_z, 0)

        def total_of(col):
            value = own(z * X + col) + take(col)
            if Z > 2:
                value = value + take(X + col)
            return value

        def to_x(j, carry):
            col = xat(j)
            sbuf_i = ZB + x
            value = total_of(col)
            sbuf[ZB + X + j] = value.astype(BF16)
            pltpu.make_async_remote_copy(
                src_ref=sbuf.at[ZB + X + j],
                dst_ref=rbuf.at[sbuf_i],
                send_sem=tsem.at[0],
                recv_sem=trsem.at[sbuf_i],
                device_id=here(z, col),
                device_id_type=MESH,
            ).start()
            return carry

        lax.fori_loop(1, X, to_x, 0)
        total = total_of(x)
        weight_sums_two()
        for dx in range(1, X):
            total = total + take(ZB + xat(dx))
        finish(total)

    @pl.when(c == 1)
    def _():
        def opposite(t, carry):
            q = last - t
            zz = (z + Z - off(q)) % Z
            put(zz, own(zz * X + xat(2)), here(z, xat(sgn(zz))))
            return carry

        lax.fori_loop(0, Z, opposite, 0)

        def beside(t, carry):
            q = last - t
            zz = (z + Z - off(q)) % Z
            sign = sgn(zz)
            against = own(zz * X + xat(-sign))
            put(2 * Z + zz, against, here(z, xat(-sign)))
            along = own(zz * X + xat(sign)) + take(zz)
            put(Z + zz, along, here(z, xat(sign)))
            return carry

        lax.fori_loop(0, Z, beside, 0)
        weight_sums_one()

        def row_total(zz):
            return own(zz * X + x) + take(Z + zz) + take(2 * Z + zz)

        def along_z(t, carry):
            q = last - t
            value = row_total((z + Z - off(q)) % Z)
            i = 3 * Z + q
            d = z_direction(q, x)
            target = here((z + Z + d) % Z, x)

            @pl.when(has_incoming(q, x))
            def _():
                put(i, value + take(3 * Z + source_q(q)), target)

            @pl.when(jnp.logical_not(has_incoming(q, x)))
            def _():
                put(i, value, target)

            return carry

        lax.fori_loop(0, Z - 1, along_z, 0)
        total = row_total(z)
        weight_sums_two()
        total = total + take(3 * Z + 1)
        if Z > 2:
            total = total + take(3 * Z + 2)
        finish(total)

    def final_copy(lp, slot, target):
        return pltpu.make_async_remote_copy(
            src_ref=fs.at[lp],
            dst_ref=fr.at[slot],
            send_sem=fsem.at[lp],
            recv_sem=frsem.at[slot],
            device_id=target,
            device_id_type=MESH,
        )

    for lp in range(2):
        is_self = jnp.logical_and(h == l, l == lp)

        @pl.when(jnp.logical_not(is_self))
        def _():
            final_copy(lp, h, (vid(l, z, x), lp * 2 + c)).start()

        @pl.when(is_self)
        def _():
            fr[h] = fs[lp]

    for dz in range(1, Z):
        src = zat(dz)
        pltpu.make_async_remote_copy(
            src_ref=g3.at[src],
            dst_ref=g3.at[src],
            send_sem=gsem.at[2],
            recv_sem=g3r.at[src],
            device_id=here(zat(dz), x),
            device_id_type=MESH,
        ).wait_recv()
    gw_ref[...] = g3[...].reshape(T, T)

    for hs in range(2):

        @pl.when(jnp.logical_not(jnp.logical_and(h == l, h == hs)))
        def _():
            final_copy(0, hs, lo_mate).wait_recv()

    both = fr[0] + fr[1]
    for ct in range(2):
        gf_ref[:, ct * T : ct * T + T] = both[ct].astype(BF16)

    for lp in range(2):

        @pl.when(jnp.logical_not(jnp.logical_and(h == l, l == lp)))
        def _():
            final_copy(lp, h, (vid(l, z, x), lp * 2 + c)).wait_send()

    first.wait_send()
    second.wait_send()
    third.wait_send()
    p_first.wait_send()
    p_second.wait_send()
    n_sent = Z * X - 1

    def drained(ref, sem):
        pltpu.make_async_remote_copy(
            src_ref=ref,
            dst_ref=ref,
            send_sem=sem,
            recv_sem=rsem.at[0],
            device_id=core_mate,
            device_id_type=MESH,
        ).wait_send()

    drained(xg.at[pl.ds(0, n_sent)], ssem.at[0])
    drained(rbuf.at[pl.ds(0, n_sent)], tsem.at[0])
    drained(g1.at[pl.ds(0, Z - 1)], gsem.at[0])
    drained(g2.at[pl.ds(0, 2 * X - 1)], gsem.at[1])
    drained(g3.at[pl.ds(0, Z - 1)], gsem.at[2])


def on_device(features, weight, bias, cotangent, adj_tiles, tile_rows, tile_cols, tile_counts):
    X = RING_X
    Z = lax.axis_size("vtx") // (2 * X)
    n_half = Z * X
    R = T // Z
    anywhere = pl.BlockSpec(memory_space=pl.ANY)
    smem = pl.BlockSpec(memory_space=pltpu.SMEM)
    vmem = pl.BlockSpec(memory_space=pltpu.VMEM)
    n_buf = 4 * Z + 2 * X
    out, gf, gw, gb = pl.pallas_call(
        functools.partial(kernel, Z),
        out_shape=(
            jax.ShapeDtypeStruct((2 * T, T), BF16),
            jax.ShapeDtypeStruct((32, 2 * T), BF16),
            jax.ShapeDtypeStruct((T, T), F32),
            jax.ShapeDtypeStruct((1, T), F32),
        ),
        in_specs=[anywhere] * 5 + [smem] * 3,
        out_specs=(vmem, vmem, vmem, vmem),
        scratch_shapes=[
            pltpu.VMEM((n_half, T, T), BF16),
            pltpu.VMEM((n_half * SLOTS, T, T), BF16),
            pltpu.VMEM((T, T), BF16),
            pltpu.VMEM((1, T), F32),
            pltpu.VMEM((2 * T, T), BF16),
            pltpu.VMEM((2, T, T), F32),
            pltpu.VMEM((2, T, T), F32),
            pltpu.VMEM((T, T), F32),
            pltpu.VMEM((2, T, T), F32),
            pltpu.VMEM((2, T, T), BF16),
            pltpu.VMEM((2, 2, 64, T), F32),
            pltpu.VMEM((2, 2, 64, T), F32),
            pltpu.VMEM((2, 64, T), F32),
            pltpu.VMEM((2, 64, T), BF16),
            pltpu.VMEM((Z, R + 8, T), F32),
            pltpu.VMEM((Z, R + 8, T), F32),
            pltpu.VMEM((R + 8, T), F32),
            pltpu.VMEM((2 * X, R + 8, T), F32),
            pltpu.VMEM((Z, R, T), F32),
            pltpu.VMEM((n_buf, T, T), BF16),
            pltpu.VMEM((n_buf, T, T), BF16),
            pltpu.VMEM((2, 2, 32, T), F32),
            pltpu.VMEM((2, 2, 32, T), F32),
            pltpu.SemaphoreType.DMA((5,)),
            pltpu.SemaphoreType.DMA((2,)),
            pltpu.SemaphoreType.DMA((n_half,)),
            pltpu.SemaphoreType.DMA((5,)),
            pltpu.SemaphoreType.DMA((5,)),
            pltpu.SemaphoreType.DMA((3,)),
            pltpu.SemaphoreType.DMA((Z,)),
            pltpu.SemaphoreType.DMA((2 * X,)),
            pltpu.SemaphoreType.DMA((Z,)),
            pltpu.SemaphoreType.DMA((1,)),
            pltpu.SemaphoreType.DMA((n_buf,)),
            pltpu.SemaphoreType.DMA((2,)),
            pltpu.SemaphoreType.DMA((2,)),
        ],
        compiler_params=pltpu.CompilerParams(
            collective_id=0, has_side_effects=True, vmem_limit_bytes=60 * 1024 * 1024
        ),
        cost_estimate=pl.CostEstimate(flops=2 * 10**9, bytes_accessed=5 * 10**6, transcendentals=32768),
    )(features, weight, bias.reshape(1, T), cotangent, adj_tiles, tile_rows.T, tile_cols.T, tile_counts)
    return out, gf.T, gw, gb.reshape(T)


def solution(mesh):
    in_specs = (
        P("vtx", None),
        P(None, "feat"),
        P("feat"),
        P("vtx", "feat"),
        P("vtx", None, None),
        P("vtx", None),
        P("vtx", None),
        P("vtx"),
    )
    out_specs = (P("vtx", "feat"), P("vtx", "feat"), P(None, "feat"), P("feat"))
    return jax.shard_map(on_device, mesh=mesh, in_specs=in_specs, out_specs=out_specs, check_vma=False)
```

```python
import functools
import math

import jax
import jax.numpy as jnp
from jax import lax
from jax.experimental import pallas as pl
from jax.experimental.pallas import tpu as pltpu
from jax.sharding import PartitionSpec as P

MESH = pl.DeviceIdType.MESH
RING_X = 4
T = 128
SLOTS = 4
F32 = jnp.float32
BF16 = jnp.bfloat16


def dot(a, b, dims=((1,), (0,))):
    return lax.dot_general(a, b, (dims, ((), ())), preferred_element_type=F32)


def split(v):
    high = v.astype(BF16)
    return high, (v - high.astype(F32)).astype(BF16)


def gelu_parts(v):
    c = math.sqrt(2.0 / math.pi)
    t = jnp.tanh(c * (v + 0.044715 * (v * v * v)))
    cdf = 0.5 * (1.0 + t)
    slope = cdf + 0.5 * v * (1.0 - t * t) * (c * (1.0 + (3.0 * 0.044715) * (v * v)))
    return v * cdf, slope


def kernel(
    Z,
    feat_h,
    weight_h,
    bias_h,
    cot_h,
    tiles_h,
    rows_h,
    cols_h,
    counts_h,
    out_ref,
    gf_ref,
    gw_ref,
    gb_ref,
    rows,
    cols,
    counts,
    mine,
    xg,
    tiles,
    w,
    bias,
    cot,
    acc,
    ex,
    sb,
    axf,
    gp,
    pt,
    pe,
    pb,
    pf,
    gwb,
    g1,
    g2s,
    g2,
    g3,
    sbuf,
    rbuf,
    fs,
    fr,
    lsem,
    ssem,
    rsem,
    exs,
    exr,
    gsem,
    g1r,
    g2r,
    g3r,
    tsem,
    trsem,
    fsem,
    frsem,
):
    X = RING_X
    E = 2 * X
    R = T // E
    NEAR = 3
    me_v = lax.axis_index("vtx")
    me_f = lax.axis_index("feat")
    h = me_v // (Z * X)
    z = (me_v // X) % Z
    x = me_v % X
    l = me_f // 2
    c = me_f % 2

    def vid(hh, zz, xx):
        return (hh * Z + zz) * X + xx

    def here(zz, xx):
        return (vid(h, zz, xx), me_f)

    core_mate = (me_v, l * 2 + 1 - c)
    lo_mate = (me_v, (1 - l) * 2 + c)

    def zat(o):
        return (z + 2 * Z + o) % Z

    def xat(o):
        return (x + X + o) % X

    def offset(q):
        return ((q + 1) // 2) * (1 - 2 * (q % 2))

    p0 = z * X + x

    half_rows = pl.ds(pl.multiple_of(c * T, T), T)
    n_half = Z * X
    tiles_copy = pltpu.make_async_copy(
        tiles_h.at[pl.ds(l * (n_half * SLOTS), n_half * SLOTS)], tiles, lsem.at[0]
    )
    w_copy = pltpu.make_async_copy(weight_h, w, lsem.at[1])
    bias_copy = pltpu.make_async_copy(bias_h, bias, lsem.at[2])
    cot_copy = pltpu.make_async_copy(cot_h, cot, lsem.at[3])
    own_copy = pltpu.make_async_copy(feat_h.at[half_rows], mine, lsem.at[4])

    index_copies = [
        pltpu.make_async_copy(src, dst, lsem.at[5 + i])
        for i, (src, dst) in enumerate(((rows_h, rows), (cols_h, cols), (counts_h, counts)))
    ]
    own_copy.start()
    for copy in index_copies:
        copy.start()
    tiles_copy.start()
    w_copy.start()
    bias_copy.start()
    cot_copy.start()

    barrier = pltpu.get_barrier_semaphore()

    def greet(v, f):
        pl.semaphore_signal(barrier, inc=1, device_id=(v, f), device_id_type=MESH)

    for q in reversed(range(1, Z)):
        zz = zat(offset(q))
        greet(vid(1 - h, zz, x), h * 2 + c)
        greet(vid(h, zz, x), h * 2 + c)

        @pl.when(h != l)
        def _():
            greet(vid(h, zz, x), me_f)

    for dx in (2, 1, 3):

        @pl.when(h != l)
        def _():
            greet(vid(1 - h, z, xat(dx)), h * 2 + c)
            greet(vid(h, z, xat(dx)), h * 2 + c)

        greet(vid(1 - h, z, xat(dx)), me_f)
        greet(vid(h, z, xat(dx)), me_f)
    greet(vid(1 - h, z, x), h * 2 + c)
    greet(*lo_mate)
    greet(*core_mate)

    @pl.when(h != l)
    def _():
        greet(vid(1 - h, z, x), me_f)

    acc[...] = jnp.zeros_like(acc)
    own_copy.wait()

    @pl.when(h == l)
    def _():
        xg[p0] = mine[...]

    n_greet = 2 * (Z - 1) + 3 * (X - 1) + 3

    @pl.when(h == l)
    def _():
        pl.semaphore_wait(barrier, n_greet)

    @pl.when(h != l)
    def _():
        pl.semaphore_wait(barrier, n_greet + Z)


    def slot_copy(p, target):
        return pltpu.make_async_remote_copy(
            src_ref=xg.at[p],
            dst_ref=xg.at[p],
            send_sem=ssem.at[0],
            recv_sem=rsem.at[p],
            device_id=target,
            device_id_type=MESH,
        )

    def wait_slot(p):
        slot_copy(p, core_mate).wait_recv()

    def first_copy(zz, xx):
        return pltpu.make_async_remote_copy(
            src_ref=mine,
            dst_ref=xg.at[p0],
            send_sem=ssem.at[0],
            recv_sem=rsem.at[p0],
            device_id=(vid(l, zz, xx), h * 2 + c),
            device_id_type=MESH,
        )

    for dx in (2, 1, 3):
        first_copy(z, xat(dx)).start()
    first_copy(zat(offset(3)), x).start()
    first_copy(zat(offset(4)), x).start()
    first_copy(zat(offset(5)), x).start()
    first_copy(zat(offset(6)), x).start()

    @pl.when(h != l)
    def _():
        first_copy(z, x).start()

    def forward(p):
        s = l * n_half + p
        count = counts[s]
        block = xg[p]
        zero = jnp.zeros_like(block)
        right = []
        for k in range(SLOTS):
            ok = jnp.logical_and(k < count, cols[k, s] == c)
            r = rows[k, s]
            right.append(
                jnp.concatenate(
                    [
                        jnp.where(jnp.logical_and(ok, r == 0), block, zero),
                        jnp.where(jnp.logical_and(ok, r == 1), block, zero),
                    ],
                    axis=1,
                )
            )
        left = jnp.concatenate([tiles[p * SLOTS + k] for k in range(SLOTS)], axis=1)
        got = dot(left, jnp.concatenate(right, axis=0))
        acc[0] += got[:, :T]
        acc[1] += got[:, T:]

    def far_row(q):
        p = zat(offset(q)) * X + x
        wait_slot(p)
        for dx in (2, 1, 3):
            slot_copy(p, here(z, xat(dx))).start()

    def arrived(q, dx):
        p = zat(offset(q)) * X + xat(dx)
        wait_slot(p)
        forward(p)

    far_row(3)
    far_row(4)
    first_copy(zat(offset(7)), x).start()
    for copy in index_copies:
        copy.wait()
    tiles_copy.wait()

    @pl.when(h != l)
    def _():
        wait_slot(p0)

    forward(p0)
    far_row(5)
    far_row(6)
    first_copy(zat(offset(1)), x).start()
    first_copy(zat(offset(2)), x).start()
    for dx in (1, 3, 2):
        p = z * X + xat(dx)
        wait_slot(p)
        slot_copy(p, here(zat(1), x)).start()
        slot_copy(p, here(zat(-1), x)).start()
    forward(zat(offset(3)) * X + x)
    forward(zat(offset(4)) * X + x)
    far_row(7)
    forward(zat(offset(5)) * X + x)
    forward(zat(offset(6)) * X + x)
    forward(zat(offset(7)) * X + x)

    def this_row(dx, carry):
        forward(z * X + xat(dx))
        return carry

    lax.fori_loop(1, X, this_row, 0)
    arrived(1, 0)
    arrived(2, 0)

    def beside(t, carry):
        arrived(t // 3 + 1, t % 3 + 1)
        return carry

    lax.fori_loop(0, 6, beside, 0)

    def far(t, carry):
        arrived(NEAR + t // 3, t % 3 + 1)
        return carry

    lax.fori_loop(0, (Z - NEAR) * 3, far, 0)

    def exchange(src, dst, i, target):
        return pltpu.make_async_remote_copy(
            src_ref=src,
            dst_ref=dst,
            send_sem=exs.at[i],
            recv_sem=exr.at[i],
            device_id=target,
            device_id_type=MESH,
        )

    first = exchange(acc.at[1 - c], ex.at[0], 0, core_mate)
    first.start()
    first.wait_recv()
    sb[...] = acc[c] + ex[0]
    second = exchange(sb, ex.at[1], 1, lo_mate)
    second.start()
    w_copy.wait()
    bias_copy.wait()
    cot_copy.wait()
    second.wait_recv()
    axf[c] = sb[...] + ex[1]
    third = exchange(axf.at[c], axf.at[c], 2, core_mate)
    third.start()

    def rows_half(r):
        high, low = split(axf[r])
        pre = dot(high, w[...]) + dot(low, w[...]) + bias[...]
        result, slope = gelu_parts(pre)
        where = pl.ds(pl.multiple_of(r * T, T), T)
        out_ref[where, :] = result.astype(BF16)
        grad = (cot[where, :].astype(F32) * slope).astype(BF16)
        gp[r] = grad
        back = dot(w[...], grad, ((1,), (1,)))
        for cc in range(2):
            for ll in range(2):
                pt[cc, r, ll * 32 : ll * 32 + 32, :] = back[ll * 64 + cc * 32 : ll * 64 + cc * 32 + 32, :]

    rows_half(c)
    exchange(axf.at[c], axf.at[1 - c], 2, core_mate).wait_recv()
    rows_half(1 - c)

    p_first = exchange(pt.at[1 - c], pe.at[0], 3, core_mate)
    p_first.start()

    local_w = jnp.zeros((T, T), F32)
    local_b = jnp.zeros((1, T), F32)
    for r in range(2):
        high, low = split(axf[r])
        grad = gp[r]
        local_w += dot(high, grad, ((0,), (0,))) + dot(low, grad, ((0,), (0,)))
        local_b += jnp.sum(grad.astype(F32), axis=0, keepdims=True)
    spread_b = jnp.broadcast_to(local_b, (8, T))
    for i in range(E):
        gwb[i, :R, :] = local_w[i * R : i * R + R, :]
        gwb[i, R:, :] = spread_b

    me_e = h * X + x

    def e_at(i):
        hh = (h + i // X) % 2
        xx = xat(i % X)
        return hh * X + xx, (vid(hh, z, xx), me_f)

    def weight_copy(src, dst, send, recv, target):
        return pltpu.make_async_remote_copy(
            src_ref=src, dst_ref=dst, send_sem=send, recv_sem=recv, device_id=target, device_id_type=MESH
        )

    for i in range(1, E):
        e, target = e_at(i)
        weight_copy(gwb.at[e], g1.at[me_e], gsem.at[0], g1r.at[me_e], target).start()

    p_first.wait_recv()
    pb[...] = pt[c] + pe[0]
    p_second = exchange(pb, pe.at[1], 4, lo_mate)
    p_second.start()
    p_second.wait_recv()
    pf[...] = (pb[...] + pe[1]).astype(BF16)

    def own(p):
        s = l * n_half + p
        count = counts[s]
        low = pf[0]
        high = pf[1]
        zero = jnp.zeros_like(low)
        left = []
        for k in range(SLOTS):
            ok = k < count
            col = cols[k, s]
            picked = jnp.where(rows[k, s] == 0, low, high)
            left.append(
                jnp.concatenate(
                    [
                        jnp.where(jnp.logical_and(ok, col == 0), picked, zero),
                        jnp.where(jnp.logical_and(ok, col == 1), picked, zero),
                    ],
                    axis=0,
                )
            )
        right = tiles[pl.ds(p * SLOTS, SLOTS)].reshape(SLOTS * T, T)
        return dot(jnp.concatenate(left, axis=1), right)

    def sum_copy(i, target):
        return pltpu.make_async_remote_copy(
            src_ref=sbuf.at[i],
            dst_ref=rbuf.at[i],
            send_sem=tsem.at[0],
            recv_sem=trsem.at[i],
            device_id=target,
            device_id_type=MESH,
        )

    def take(i):
        sum_copy(i, core_mate).wait_recv()
        return rbuf[i].astype(F32)

    def put(i, value, target):
        sbuf[i] = value.astype(BF16)
        sum_copy(i, target).start()

    def weight_sums_one():
        total = gwb[me_e]
        for i in range(1, E):
            e, target = e_at(i)
            weight_copy(gwb.at[e], g1.at[e], gsem.at[0], g1r.at[e], target).wait_recv()
            total = total + g1[e]
        g2s[...] = total
        for dz in range(1, Z):
            weight_copy(g2s, g2.at[z], gsem.at[1], g2r.at[z], here(zat(dz), x)).start()

    def weight_sums_two():
        total = g2s[...]
        for dz in range(1, Z):
            zz = zat(dz)
            weight_copy(g2s, g2.at[zz], gsem.at[1], g2r.at[zz], here(zz, x)).wait_recv()
            total = total + g2[zz]
        g3[me_e] = total[:R, :]
        gb_ref[...] = total[R : R + 1, :]
        for i in range(1, E):
            e, target = e_at(i)
            weight_copy(g3.at[me_e], g3.at[me_e], gsem.at[2], g3r.at[me_e], target).start()

    def row_to(q):
        return zat(-offset(q))

    NS = Z + X - 1

    def final_copy(i, lp, slot, target):
        return pltpu.make_async_remote_copy(
            src_ref=fs.at[i, lp],
            dst_ref=fr.at[slot],
            send_sem=fsem.at[0],
            recv_sem=frsem.at[slot],
            device_id=target,
            device_id_type=MESH,
        )

    def deliver(value, i, zz, xx):
        value = value.astype(BF16)
        for lp in range(2):
            for ct in range(2):
                fs[i, lp, ct] = value[ct * 64 + lp * 32 : ct * 64 + lp * 32 + 32, :]
            is_self = jnp.logical_and(jnp.logical_and(h == l, l == lp), i == 0)

            @pl.when(jnp.logical_not(is_self))
            def _():
                final_copy(i, lp, h * NS + i, (vid(l, zz, xx), lp * 2 + c)).start()

            @pl.when(is_self)
            def _():
                fr[h * NS + i] = fs[i, lp]

    def far_x(t, carry):
        zz = row_to(Z - 1 - t)
        for dx in (2, 1, 3):
            put(zz * 3 + dx - 1, own(zz * X + xat(dx)), here(z, xat(dx)))
        return carry

    def beside_z(t, carry):
        q, dx = t // 3 + 1, t % 3 + 1
        zz = row_to(q)
        put(3 * Z + t, own(zz * X + xat(dx)), here(zz, x))
        return carry

    def both_ways(t, carry):
        far_x(t, carry)
        return beside_z(t, carry)

    first_part = min(Z - NEAR, 6)
    lax.fori_loop(0, first_part, both_ways, 0)
    lax.fori_loop(first_part, Z - NEAR, far_x, 0)
    lax.fori_loop(first_part, 6, beside_z, 0)

    def same_column(q, carry):
        zz = row_to(q)
        deliver(own(zz * X + x), q, zz, x)
        return carry

    lax.fori_loop(0, NEAR, same_column, 0)
    weight_sums_one()

    def this_row_x(dx, carry):
        value = own(z * X + xat(dx)) + take(3 * Z + dx - 1) + take(3 * Z + 3 + dx - 1)
        deliver(value, Z - 1 + dx, z, xat(dx))
        return carry

    lax.fori_loop(1, X, this_row_x, 0)

    def far_z(t, carry):
        q = Z - 1 - t
        zz = row_to(q)
        value = own(zz * X + x)
        for dx in (1, 3, 2):
            value = value + take(zz * 3 + dx - 1)
        deliver(value, q, zz, x)
        return carry

    lax.fori_loop(0, Z - NEAR, far_z, 0)
    weight_sums_two()

    def collect(slot, total):
        is_self = jnp.logical_and(h == l, slot == h * NS)

        @pl.when(jnp.logical_not(is_self))
        def _():
            final_copy(0, 0, slot, core_mate).wait_recv()

        return total + fr[slot].astype(F32)

    both = lax.fori_loop(0, 2 * NS, collect, jnp.zeros((2, 32, T), F32))
    for ct in range(2):
        gf_ref[:, ct * T : ct * T + T] = both[ct].astype(BF16)

    for i in range(1, E):
        e, target = e_at(i)
        weight_copy(g3.at[e], g3.at[e], gsem.at[2], g3r.at[e], target).wait_recv()
    gw_ref[...] = g3[...].reshape(T, T)

    first.wait_send()
    second.wait_send()
    third.wait_send()
    p_first.wait_send()
    p_second.wait_send()
    n_sent = Z * X - 1

    def drained(ref, sem):
        pltpu.make_async_remote_copy(
            src_ref=ref,
            dst_ref=ref,
            send_sem=sem,
            recv_sem=rsem.at[0],
            device_id=core_mate,
            device_id_type=MESH,
        ).wait_send()

    drained(xg.at[pl.ds(0, n_sent)], ssem.at[0])
    drained(rbuf.at[pl.ds(0, 3 * (Z - NEAR) + 6)], tsem.at[0])
    drained(fr.at[pl.ds(0, 2 * NS - 1)], fsem.at[0])

    @pl.when(h != l)
    def _():
        drained(mine, ssem.at[0])
        drained(fr.at[0], fsem.at[0])

    drained(g1.at[pl.ds(0, E - 1)], gsem.at[0])
    drained(g2.at[pl.ds(0, Z - 1)], gsem.at[1])
    drained(g3.at[pl.ds(0, E - 1)], gsem.at[2])


def write_out(*refs):
    for source, target in zip(refs[:4], refs[4:]):
        target[...] = source[...]


def on_device(features, weight, bias, cotangent, adj_tiles, tile_rows, tile_cols, tile_counts):
    X = RING_X
    Z = lax.axis_size("vtx") // (2 * X)
    n_half = Z * X
    E = 2 * X
    R = T // E
    n_final = Z + X - 1
    anywhere = pl.BlockSpec(memory_space=pl.ANY)
    vmem = pl.BlockSpec(memory_space=pltpu.VMEM)
    n_buf = 3 * Z + 6
    out, gf, gw, gb = pl.pallas_call(
        functools.partial(kernel, Z),
        out_shape=(
            jax.ShapeDtypeStruct((2 * T, T), BF16),
            jax.ShapeDtypeStruct((32, 2 * T), BF16),
            jax.ShapeDtypeStruct((T, T), F32),
            jax.ShapeDtypeStruct((1, T), F32),
        ),
        in_specs=[anywhere] * 8,
        out_specs=(vmem, vmem, vmem, vmem),
        scratch_shapes=[
            pltpu.SMEM((SLOTS, 2 * n_half), jnp.int32),
            pltpu.SMEM((SLOTS, 2 * n_half), jnp.int32),
            pltpu.SMEM((2 * n_half,), jnp.int32),
            pltpu.VMEM((T, T), BF16),
            pltpu.VMEM((n_half, T, T), BF16),
            pltpu.VMEM((n_half * SLOTS, T, T), BF16),
            pltpu.VMEM((T, T), BF16),
            pltpu.VMEM((1, T), F32),
            pltpu.VMEM((2 * T, T), BF16),
            pltpu.VMEM((2, T, T), F32),
            pltpu.VMEM((2, T, T), F32),
            pltpu.VMEM((T, T), F32),
            pltpu.VMEM((2, T, T), F32),
            pltpu.VMEM((2, T, T), BF16),
            pltpu.VMEM((2, 2, 64, T), F32),
            pltpu.VMEM((2, 2, 64, T), F32),
            pltpu.VMEM((2, 64, T), F32),
            pltpu.VMEM((2, 64, T), BF16),
            pltpu.VMEM((E, R + 8, T), F32),
            pltpu.VMEM((E, R + 8, T), F32),
            pltpu.VMEM((R + 8, T), F32),
            pltpu.VMEM((Z, R + 8, T), F32),
            pltpu.VMEM((E, R, T), F32),
            pltpu.VMEM((n_buf, T, T), BF16),
            pltpu.VMEM((n_buf, T, T), BF16),
            pltpu.VMEM((n_final, 2, 2, 32, T), BF16),
            pltpu.VMEM((2 * n_final, 2, 32, T), BF16),
            pltpu.SemaphoreType.DMA((8,)),
            pltpu.SemaphoreType.DMA((1,)),
            pltpu.SemaphoreType.DMA((n_half,)),
            pltpu.SemaphoreType.DMA((5,)),
            pltpu.SemaphoreType.DMA((5,)),
            pltpu.SemaphoreType.DMA((3,)),
            pltpu.SemaphoreType.DMA((E,)),
            pltpu.SemaphoreType.DMA((Z,)),
            pltpu.SemaphoreType.DMA((E,)),
            pltpu.SemaphoreType.DMA((1,)),
            pltpu.SemaphoreType.DMA((n_buf,)),
            pltpu.SemaphoreType.DMA((1,)),
            pltpu.SemaphoreType.DMA((2 * n_final,)),
        ],
        compiler_params=pltpu.CompilerParams(
            collective_id=0, has_side_effects=True, vmem_limit_bytes=60 * 1024 * 1024
        ),
        cost_estimate=pl.CostEstimate(flops=2 * 10**9, bytes_accessed=5 * 10**6, transcendentals=32768),
    )(features, weight, bias.reshape(1, T), cotangent, adj_tiles, tile_rows.T, tile_cols.T, tile_counts)
    results = (out, gf, gw, gb)
    out, gf, gw, gb = pl.pallas_call(
        write_out,
        out_shape=tuple(jax.ShapeDtypeStruct(a.shape, a.dtype) for a in results),
        in_specs=[vmem] * 4,
        out_specs=(vmem,) * 4,
    )(*results)
    return out, gf.T, gw, gb.reshape(T)


def solution(mesh):
    in_specs = (
        P("vtx", None),
        P(None, "feat"),
        P("feat"),
        P("vtx", "feat"),
        P("vtx", None, None),
        P("vtx", None),
        P("vtx", None),
        P("vtx"),
    )
    out_specs = (P("vtx", "feat"), P("vtx", "feat"), P(None, "feat"), P("feat"))
    return jax.shard_map(on_device, mesh=mesh, in_specs=in_specs, out_specs=out_specs, check_vma=False)
```

```python
import functools
import math

import jax
import jax.numpy as jnp
from jax import lax
from jax.experimental import pallas as pl
from jax.experimental.pallas import tpu as pltpu
from jax.sharding import PartitionSpec as P

MESH = pl.DeviceIdType.MESH
RING_X = 4
T = 128
SLOTS = 4
F32 = jnp.float32
BF16 = jnp.bfloat16


def dot(a, b, dims=((1,), (0,))):
    return lax.dot_general(a, b, (dims, ((), ())), preferred_element_type=F32)


def split(v):
    high = v.astype(BF16)
    return high, (v - high.astype(F32)).astype(BF16)


def gelu_parts(v):
    c = math.sqrt(2.0 / math.pi)
    t = jnp.tanh(c * (v + 0.044715 * (v * v * v)))
    cdf = 0.5 * (1.0 + t)
    slope = cdf + 0.5 * v * (1.0 - t * t) * (c * (1.0 + (3.0 * 0.044715) * (v * v)))
    return v * cdf, slope


def kernel(
    Z,
    feat_h,
    weight_h,
    bias_h,
    cot_h,
    tiles_h,
    rows_h,
    cols_h,
    counts_h,
    out_ref,
    gf_ref,
    gw_ref,
    gb_ref,
    rows,
    cols,
    counts,
    mine,
    xg,
    tiles,
    w,
    bias,
    cot,
    acc,
    ex,
    sb,
    axf,
    gp,
    pt,
    pe,
    pb,
    pq,
    pf,
    gwb,
    g1,
    g2s,
    g2,
    g3,
    sbuf,
    rbuf,
    fs,
    fr,
    lsem,
    ssem,
    rsem,
    exs,
    exr,
    gsem,
    g1r,
    g2r,
    g3r,
    tsem,
    trsem,
    fsem,
    frsem,
):
    X = RING_X
    E = 2 * X
    R = T // E
    NEAR = 3
    WIDE = 5
    me_v = lax.axis_index("vtx")
    me_f = lax.axis_index("feat")
    h = me_v // (Z * X)
    z = (me_v // X) % Z
    x = me_v % X
    l = me_f // 2
    c = me_f % 2

    def vid(hh, zz, xx):
        return (hh * Z + zz) * X + xx

    def here(zz, xx):
        return (vid(h, zz, xx), me_f)

    core_mate = (me_v, l * 2 + 1 - c)
    lo_mate = (me_v, (1 - l) * 2 + c)

    def zat(o):
        return (z + 2 * Z + o) % Z

    def xat(o):
        return (x + X + o) % X

    def offset(q):
        return ((q + 1) // 2) * (1 - 2 * (q % 2))

    p0 = z * X + x

    half_rows = pl.ds(pl.multiple_of(c * T, T), T)
    n_half = Z * X
    tiles_copy = pltpu.make_async_copy(
        tiles_h.at[pl.ds(l * (n_half * SLOTS), n_half * SLOTS)], tiles, lsem.at[0]
    )
    w_copy = pltpu.make_async_copy(weight_h, w, lsem.at[1])
    bias_copy = pltpu.make_async_copy(bias_h, bias, lsem.at[2])
    cot_copy = pltpu.make_async_copy(cot_h, cot, lsem.at[3])
    own_copy = pltpu.make_async_copy(feat_h.at[half_rows], mine, lsem.at[4])

    index_copies = [
        pltpu.make_async_copy(src, dst, lsem.at[5 + i])
        for i, (src, dst) in enumerate(((rows_h, rows), (cols_h, cols), (counts_h, counts)))
    ]
    own_copy.start()
    for copy in index_copies:
        copy.start()
    tiles_copy.start()
    w_copy.start()
    bias_copy.start()
    cot_copy.start()

    barrier = pltpu.get_barrier_semaphore()

    def greet(v, f):
        pl.semaphore_signal(barrier, inc=1, device_id=(v, f), device_id_type=MESH)

    for q in reversed(range(1, Z)):
        zz = zat(offset(q))
        greet(vid(1 - h, zz, x), h * 2 + c)
        greet(vid(h, zz, x), h * 2 + c)

        @pl.when(h != l)
        def _():
            greet(vid(h, zz, x), me_f)

    for dx in (2, 1, 3):

        @pl.when(h != l)
        def _():
            greet(vid(1 - h, z, xat(dx)), h * 2 + c)
            greet(vid(h, z, xat(dx)), h * 2 + c)

        greet(vid(1 - h, z, xat(dx)), me_f)
        greet(vid(h, z, xat(dx)), me_f)
    greet(vid(1 - h, z, x), h * 2 + c)
    greet(*lo_mate)
    greet(*core_mate)

    @pl.when(h != l)
    def _():
        greet(vid(1 - h, z, x), me_f)

    acc[...] = jnp.zeros_like(acc)
    own_copy.wait()

    @pl.when(h == l)
    def _():
        xg[p0] = mine[...]

    n_greet = 2 * (Z - 1) + 3 * (X - 1) + 3

    @pl.when(h == l)
    def _():
        pl.semaphore_wait(barrier, n_greet)

    @pl.when(h != l)
    def _():
        pl.semaphore_wait(barrier, n_greet + Z)


    def slot_copy(p, target):
        return pltpu.make_async_remote_copy(
            src_ref=xg.at[p],
            dst_ref=xg.at[p],
            send_sem=ssem.at[0],
            recv_sem=rsem.at[p],
            device_id=target,
            device_id_type=MESH,
        )

    def wait_slot(p):
        slot_copy(p, core_mate).wait_recv()

    def first_copy(zz, xx):
        return pltpu.make_async_remote_copy(
            src_ref=mine,
            dst_ref=xg.at[p0],
            send_sem=ssem.at[0],
            recv_sem=rsem.at[p0],
            device_id=(vid(l, zz, xx), h * 2 + c),
            device_id_type=MESH,
        )

    for dx in (2, 1, 3):
        first_copy(z, xat(dx)).start()
    first_copy(zat(offset(3)), x).start()
    first_copy(zat(offset(4)), x).start()
    first_copy(zat(offset(5)), x).start()
    first_copy(zat(offset(6)), x).start()

    @pl.when(h != l)
    def _():
        first_copy(z, x).start()

    def forward(p):
        s = l * n_half + p
        count = counts[s]
        block = xg[p]
        zero = jnp.zeros_like(block)
        right = []
        for k in range(SLOTS):
            ok = jnp.logical_and(k < count, cols[k, s] == c)
            r = rows[k, s]
            right.append(
                jnp.concatenate(
                    [
                        jnp.where(jnp.logical_and(ok, r == 0), block, zero),
                        jnp.where(jnp.logical_and(ok, r == 1), block, zero),
                    ],
                    axis=1,
                )
            )
        left = jnp.concatenate([tiles[p * SLOTS + k] for k in range(SLOTS)], axis=1)
        got = dot(left, jnp.concatenate(right, axis=0))
        acc[0] += got[:, :T]
        acc[1] += got[:, T:]

    def far_row(q):
        p = zat(offset(q)) * X + x
        wait_slot(p)
        for dx in (1, 3) if q < WIDE else (2, 1, 3):
            slot_copy(p, here(z, xat(dx))).start()

    def arrived(q, dx):
        p = zat(offset(q)) * X + xat(dx)
        wait_slot(p)
        forward(p)

    for dx in (1, 3, 2):
        p = z * X + xat(dx)
        wait_slot(p)
        if dx == 2:
            slot_copy(p, here(zat(2), x)).start()
            slot_copy(p, here(zat(-2), x)).start()
        slot_copy(p, here(zat(1), x)).start()
        slot_copy(p, here(zat(-1), x)).start()
    far_row(3)
    far_row(4)
    first_copy(zat(offset(7)), x).start()
    for copy in index_copies:
        copy.wait()
    tiles_copy.wait()

    @pl.when(h != l)
    def _():
        wait_slot(p0)

    forward(p0)
    far_row(5)
    far_row(6)
    first_copy(zat(offset(1)), x).start()
    first_copy(zat(offset(2)), x).start()
    forward(zat(offset(3)) * X + x)
    forward(zat(offset(4)) * X + x)
    far_row(7)
    forward(zat(offset(5)) * X + x)
    forward(zat(offset(6)) * X + x)
    forward(zat(offset(7)) * X + x)

    def this_row(dx, carry):
        forward(z * X + xat(dx))
        return carry

    lax.fori_loop(1, X, this_row, 0)
    arrived(1, 0)
    arrived(2, 0)

    def beside(t, carry):
        arrived(t // 3 + 1, t % 3 + 1)
        return carry

    lax.fori_loop(0, 6, beside, 0)

    def far(t, carry):
        arrived(NEAR + t // 3, t % 3 + 1)
        return carry

    lax.fori_loop(0, (Z - NEAR) * 3, far, 0)

    def exchange(src, dst, i, target):
        return pltpu.make_async_remote_copy(
            src_ref=src,
            dst_ref=dst,
            send_sem=exs.at[i],
            recv_sem=exr.at[i],
            device_id=target,
            device_id_type=MESH,
        )

    first = exchange(acc.at[1 - c], ex.at[0], 0, core_mate)
    first.start()
    first.wait_recv()
    sb[...] = acc[c] + ex[0]
    second = exchange(sb, ex.at[1], 1, lo_mate)
    second.start()
    w_copy.wait()
    bias_copy.wait()
    cot_copy.wait()
    second.wait_recv()
    axf[c] = sb[...] + ex[1]
    third = exchange(axf.at[c], axf.at[c], 2, core_mate)
    third.start()

    def rows_half(r):
        high, low = split(axf[r])
        pre = dot(high, w[...]) + dot(low, w[...]) + bias[...]
        result, slope = gelu_parts(pre)
        where = pl.ds(pl.multiple_of(r * T, T), T)
        out_ref[where, :] = result.astype(BF16)
        grad = (cot[where, :].astype(F32) * slope).astype(BF16)
        gp[r] = grad
        back = dot(w[...], grad, ((1,), (1,)))
        for cc in range(2):
            for ll in range(2):
                pt[cc, r, ll * 32 : ll * 32 + 32, :] = back[ll * 64 + cc * 32 : ll * 64 + cc * 32 + 32, :]

    rows_half(c)
    exchange(axf.at[c], axf.at[1 - c], 2, core_mate).wait_recv()
    rows_half(1 - c)

    p_first = exchange(pt.at[1 - c], pe.at[0], 3, core_mate)
    p_first.start()

    local_w = jnp.zeros((T, T), F32)
    local_b = jnp.zeros((1, T), F32)
    for r in range(2):
        high, low = split(axf[r])
        grad = gp[r]
        local_w += dot(high, grad, ((0,), (0,))) + dot(low, grad, ((0,), (0,)))
        local_b += jnp.sum(grad.astype(F32), axis=0, keepdims=True)
    spread_b = jnp.broadcast_to(local_b, (8, T))
    for i in range(E):
        gwb[i, :R, :] = local_w[i * R : i * R + R, :]
        gwb[i, R:, :] = spread_b

    me_e = h * X + x

    def e_at(i):
        hh = (h + i // X) % 2
        xx = xat(i % X)
        return hh * X + xx, (vid(hh, z, xx), me_f)

    def weight_copy(src, dst, send, recv, target):
        return pltpu.make_async_remote_copy(
            src_ref=src, dst_ref=dst, send_sem=send, recv_sem=recv, device_id=target, device_id_type=MESH
        )

    for i in range(1, E):
        e, target = e_at(i)
        weight_copy(gwb.at[e], g1.at[me_e], gsem.at[0], g1r.at[me_e], target).start()

    p_first.wait_recv()
    chip_p = pt[c] + pe[0]
    pb[...] = chip_p.astype(BF16)
    p_second = exchange(pb, pq, 4, lo_mate)
    p_second.start()
    p_second.wait_recv()
    pf[...] = (chip_p + pq[...].astype(F32)).astype(BF16)

    def own(p):
        s = l * n_half + p
        count = counts[s]
        low = pf[0]
        high = pf[1]
        zero = jnp.zeros_like(low)
        left = []
        for k in range(SLOTS):
            ok = k < count
            col = cols[k, s]
            picked = jnp.where(rows[k, s] == 0, low, high)
            left.append(
                jnp.concatenate(
                    [
                        jnp.where(jnp.logical_and(ok, col == 0), picked, zero),
                        jnp.where(jnp.logical_and(ok, col == 1), picked, zero),
                    ],
                    axis=0,
                )
            )
        right = tiles[pl.ds(p * SLOTS, SLOTS)].reshape(SLOTS * T, T)
        return dot(jnp.concatenate(left, axis=1), right)

    def sum_copy(i, target):
        return pltpu.make_async_remote_copy(
            src_ref=sbuf.at[i],
            dst_ref=rbuf.at[i],
            send_sem=tsem.at[0],
            recv_sem=trsem.at[i],
            device_id=target,
            device_id_type=MESH,
        )

    def take(i):
        sum_copy(i, core_mate).wait_recv()
        return rbuf[i].astype(F32)

    def put(i, value, target):
        sbuf[i] = value.astype(BF16)
        sum_copy(i, target).start()

    def weight_sums_one():
        total = gwb[me_e]
        for i in range(1, E):
            e, target = e_at(i)
            weight_copy(gwb.at[e], g1.at[e], gsem.at[0], g1r.at[e], target).wait_recv()
            total = total + g1[e]
        g2s[...] = total
        for dz in range(1, Z):
            weight_copy(g2s, g2.at[z], gsem.at[1], g2r.at[z], here(zat(dz), x)).start()

    def weight_sums_two():
        total = g2s[...]
        for dz in range(1, Z):
            zz = zat(dz)
            weight_copy(g2s, g2.at[zz], gsem.at[1], g2r.at[zz], here(zz, x)).wait_recv()
            total = total + g2[zz]
        g3[me_e] = total[:R, :]
        gb_ref[...] = total[R : R + 1, :]
        for i in range(1, E):
            e, target = e_at(i)
            weight_copy(g3.at[me_e], g3.at[me_e], gsem.at[2], g3r.at[me_e], target).start()

    def row_to(q):
        return zat(-offset(q))

    NS = Z + X - 1

    def final_copy(i, lp, slot, target):
        return pltpu.make_async_remote_copy(
            src_ref=fs.at[i, lp],
            dst_ref=fr.at[slot],
            send_sem=fsem.at[0],
            recv_sem=frsem.at[slot],
            device_id=target,
            device_id_type=MESH,
        )

    def deliver(value, i, zz, xx):
        value = value.astype(BF16)
        for lp in range(2):
            for ct in range(2):
                fs[i, lp, ct] = value[ct * 64 + lp * 32 : ct * 64 + lp * 32 + 32, :]
            is_self = jnp.logical_and(jnp.logical_and(h == l, l == lp), i == 0)

            @pl.when(jnp.logical_not(is_self))
            def _():
                final_copy(i, lp, h * NS + i, (vid(l, zz, xx), lp * 2 + c)).start()

            @pl.when(is_self)
            def _():
                fr[h * NS + i] = fs[i, lp]

    def far_x(q):
        zz = row_to(q)
        for dx in (1, 3) if q < WIDE else (2, 1, 3):
            put(zz * 3 + dx - 1, own(zz * X + xat(dx)), here(z, xat(dx)))

    def beside_z(q, dx):
        zz = row_to(q)
        put(3 * Z + (q - 1) * 3 + dx - 1, own(zz * X + xat(dx)), here(zz, x))

    beside = [(3, 2), (4, 2), (1, 1), (2, 1), (1, 2), (2, 2), (1, 3), (2, 3)]
    for q in reversed(range(NEAR, Z)):
        far_x(q)
        for _ in range(2):
            if beside:
                beside_z(*beside.pop(0))

    def same_column(q, carry):
        zz = row_to(q)
        deliver(own(zz * X + x), q, zz, x)
        return carry

    weight_sums_one()

    def this_row_x(dx):
        value = own(z * X + xat(dx)) + take(3 * Z + dx - 1) + take(3 * Z + 3 + dx - 1)
        if dx == 2:
            value = value + take(3 * Z + 6 + dx - 1) + take(3 * Z + 9 + dx - 1)
        deliver(value, Z - 1 + dx, z, xat(dx))


    def far_z(q):
        zz = row_to(q)
        value = own(zz * X + x)
        for dx in (1, 3) if q < WIDE else (1, 3, 2):
            value = value + take(zz * 3 + dx - 1)
        deliver(value, q, zz, x)

    for q in reversed(range(NEAR, Z)):
        far_z(q)
    for dx in (1, 3, 2):
        this_row_x(dx)
    lax.fori_loop(0, NEAR, same_column, 0)
    weight_sums_two()

    def collect(slot, total):
        is_self = jnp.logical_and(h == l, slot == h * NS)

        @pl.when(jnp.logical_not(is_self))
        def _():
            final_copy(0, 0, slot, core_mate).wait_recv()

        return total + fr[slot].astype(F32)

    both = lax.fori_loop(0, 2 * NS, collect, jnp.zeros((2, 32, T), F32))
    for ct in range(2):
        gf_ref[:, ct * T : ct * T + T] = both[ct].astype(BF16)

    for i in range(1, E):
        e, target = e_at(i)
        weight_copy(g3.at[e], g3.at[e], gsem.at[2], g3r.at[e], target).wait_recv()
    gw_ref[...] = g3[...].reshape(T, T)

    first.wait_send()
    second.wait_send()
    third.wait_send()
    p_first.wait_send()
    p_second.wait_send()
    n_sent = Z * X - 1

    def drained(ref, sem):
        pltpu.make_async_remote_copy(
            src_ref=ref,
            dst_ref=ref,
            send_sem=sem,
            recv_sem=rsem.at[0],
            device_id=core_mate,
            device_id_type=MESH,
        ).wait_send()

    drained(xg.at[pl.ds(0, n_sent)], ssem.at[0])
    drained(rbuf.at[pl.ds(0, 3 * (Z - NEAR) + 6)], tsem.at[0])
    drained(fr.at[pl.ds(0, 2 * NS - 1)], fsem.at[0])

    @pl.when(h != l)
    def _():
        drained(mine, ssem.at[0])
        drained(fr.at[0], fsem.at[0])

    drained(g1.at[pl.ds(0, E - 1)], gsem.at[0])
    drained(g2.at[pl.ds(0, Z - 1)], gsem.at[1])
    drained(g3.at[pl.ds(0, E - 1)], gsem.at[2])


def write_out(*refs):
    for source, target in zip(refs[:4], refs[4:]):
        target[...] = source[...]


def on_device(features, weight, bias, cotangent, adj_tiles, tile_rows, tile_cols, tile_counts):
    X = RING_X
    Z = lax.axis_size("vtx") // (2 * X)
    n_half = Z * X
    E = 2 * X
    R = T // E
    n_final = Z + X - 1
    anywhere = pl.BlockSpec(memory_space=pl.ANY)
    vmem = pl.BlockSpec(memory_space=pltpu.VMEM)
    n_buf = 3 * Z + 12
    out, gf, gw, gb = pl.pallas_call(
        functools.partial(kernel, Z),
        out_shape=(
            jax.ShapeDtypeStruct((2 * T, T), BF16),
            jax.ShapeDtypeStruct((32, 2 * T), BF16),
            jax.ShapeDtypeStruct((T, T), F32),
            jax.ShapeDtypeStruct((1, T), F32),
        ),
        in_specs=[anywhere] * 8,
        out_specs=(vmem, vmem, vmem, vmem),
        scratch_shapes=[
            pltpu.SMEM((SLOTS, 2 * n_half), jnp.int32),
            pltpu.SMEM((SLOTS, 2 * n_half), jnp.int32),
            pltpu.SMEM((2 * n_half,), jnp.int32),
            pltpu.VMEM((T, T), BF16),
            pltpu.VMEM((n_half, T, T), BF16),
            pltpu.VMEM((n_half * SLOTS, T, T), BF16),
            pltpu.VMEM((T, T), BF16),
            pltpu.VMEM((1, T), F32),
            pltpu.VMEM((2 * T, T), BF16),
            pltpu.VMEM((2, T, T), F32),
            pltpu.VMEM((2, T, T), F32),
            pltpu.VMEM((T, T), F32),
            pltpu.VMEM((2, T, T), F32),
            pltpu.VMEM((2, T, T), BF16),
            pltpu.VMEM((2, 2, 64, T), F32),
            pltpu.VMEM((1, 2, 64, T), F32),
            pltpu.VMEM((2, 64, T), BF16),
            pltpu.VMEM((2, 64, T), BF16),
            pltpu.VMEM((2, 64, T), BF16),
            pltpu.VMEM((E, R + 8, T), F32),
            pltpu.VMEM((E, R + 8, T), F32),
            pltpu.VMEM((R + 8, T), F32),
            pltpu.VMEM((Z, R + 8, T), F32),
            pltpu.VMEM((E, R, T), F32),
            pltpu.VMEM((n_buf, T, T), BF16),
            pltpu.VMEM((n_buf, T, T), BF16),
            pltpu.VMEM((n_final, 2, 2, 32, T), BF16),
            pltpu.VMEM((2 * n_final, 2, 32, T), BF16),
            pltpu.SemaphoreType.DMA((8,)),
            pltpu.SemaphoreType.DMA((1,)),
            pltpu.SemaphoreType.DMA((n_half,)),
            pltpu.SemaphoreType.DMA((5,)),
            pltpu.SemaphoreType.DMA((5,)),
            pltpu.SemaphoreType.DMA((3,)),
            pltpu.SemaphoreType.DMA((E,)),
            pltpu.SemaphoreType.DMA((Z,)),
            pltpu.SemaphoreType.DMA((E,)),
            pltpu.SemaphoreType.DMA((1,)),
            pltpu.SemaphoreType.DMA((n_buf,)),
            pltpu.SemaphoreType.DMA((1,)),
            pltpu.SemaphoreType.DMA((2 * n_final,)),
        ],
        compiler_params=pltpu.CompilerParams(
            collective_id=0, has_side_effects=True, vmem_limit_bytes=60 * 1024 * 1024
        ),
        cost_estimate=pl.CostEstimate(flops=2 * 10**9, bytes_accessed=5 * 10**6, transcendentals=32768),
    )(features, weight, bias.reshape(1, T), cotangent, adj_tiles, tile_rows.T, tile_cols.T, tile_counts)
    results = (out, gf, gw, gb)
    out, gf, gw, gb = pl.pallas_call(
        write_out,
        out_shape=tuple(jax.ShapeDtypeStruct(a.shape, a.dtype) for a in results),
        in_specs=[vmem] * 4,
        out_specs=(vmem,) * 4,
    )(*results)
    return out, gf.T, gw, gb.reshape(T)


def solution(mesh):
    in_specs = (
        P("vtx", None),
        P(None, "feat"),
        P("feat"),
        P("vtx", "feat"),
        P("vtx", None, None),
        P("vtx", None),
        P("vtx", None),
        P("vtx"),
    )
    out_specs = (P("vtx", "feat"), P("vtx", "feat"), P(None, "feat"), P("feat"))
    return jax.shard_map(on_device, mesh=mesh, in_specs=in_specs, out_specs=out_specs, check_vma=False)
```

```python
import functools
import math

import jax
import jax.numpy as jnp
from jax import lax
from jax.experimental import pallas as pl
from jax.experimental.pallas import tpu as pltpu
from jax.sharding import PartitionSpec as P

MESH = pl.DeviceIdType.MESH
RING_X = 4
T = 128
SLOTS = 4
F32 = jnp.float32
BF16 = jnp.bfloat16


def dot(a, b, dims=((1,), (0,))):
    return lax.dot_general(a, b, (dims, ((), ())), preferred_element_type=F32)


def split(v):
    high = v.astype(BF16)
    return high, (v - high.astype(F32)).astype(BF16)


def gelu_parts(v):
    c = math.sqrt(2.0 / math.pi)
    t = jnp.tanh(c * (v + 0.044715 * (v * v * v)))
    cdf = 0.5 * (1.0 + t)
    slope = cdf + 0.5 * v * (1.0 - t * t) * (c * (1.0 + (3.0 * 0.044715) * (v * v)))
    return v * cdf, slope


def kernel(
    Z,
    feat_h,
    weight_h,
    bias_h,
    cot_h,
    tiles_h,
    rows_h,
    cols_h,
    counts_h,
    out_ref,
    gf_ref,
    gw_ref,
    gb_ref,
    rows,
    cols,
    counts,
    mine,
    xg,
    tiles,
    w,
    bias,
    cot,
    acc,
    ex,
    sb,
    axf,
    gp,
    pt,
    pe,
    pb,
    pq,
    pf,
    gwb,
    g1,
    g2s,
    g2,
    g3,
    sbuf,
    rbuf,
    fs,
    fr,
    lsem,
    ssem,
    rsem,
    exs,
    exr,
    gsem,
    g1r,
    g2r,
    g3r,
    tsem,
    trsem,
    fsem,
    frsem,
):
    X = RING_X
    E = 2 * X
    R = T // E
    NEAR = 3
    WIDE = 5
    me_v = lax.axis_index("vtx")
    me_f = lax.axis_index("feat")
    h = me_v // (Z * X)
    z = (me_v // X) % Z
    x = me_v % X
    l = me_f // 2
    c = me_f % 2

    def vid(hh, zz, xx):
        return (hh * Z + zz) * X + xx

    def here(zz, xx):
        return (vid(h, zz, xx), me_f)

    core_mate = (me_v, l * 2 + 1 - c)
    lo_mate = (me_v, (1 - l) * 2 + c)

    mirror = 1 - 2 * c

    def zat(o):
        return (z + 2 * Z + mirror * o) % Z

    def xat(o):
        return (x + X + mirror * o) % X

    def offset(q):
        return ((q + 1) // 2) * (1 - 2 * (q % 2))

    p0 = z * X + x

    half_rows = pl.ds(pl.multiple_of(c * T, T), T)
    n_half = Z * X
    tiles_copy = pltpu.make_async_copy(
        tiles_h.at[pl.ds(l * (n_half * SLOTS), n_half * SLOTS)], tiles, lsem.at[0]
    )
    w_copy = pltpu.make_async_copy(weight_h, w, lsem.at[1])
    bias_copy = pltpu.make_async_copy(bias_h, bias, lsem.at[2])
    cot_copy = pltpu.make_async_copy(cot_h, cot, lsem.at[3])
    own_copy = pltpu.make_async_copy(feat_h.at[half_rows], mine, lsem.at[4])

    index_copies = [
        pltpu.make_async_copy(src, dst, lsem.at[5 + i])
        for i, (src, dst) in enumerate(((rows_h, rows), (cols_h, cols), (counts_h, counts)))
    ]
    own_copy.start()
    for copy in index_copies:
        copy.start()
    tiles_copy.start()
    w_copy.start()
    bias_copy.start()
    cot_copy.start()

    barrier = pltpu.get_barrier_semaphore()

    def greet(v, f):
        pl.semaphore_signal(barrier, inc=1, device_id=(v, f), device_id_type=MESH)

    for q in reversed(range(1, Z)):
        zz = zat(offset(q))
        greet(vid(1 - h, zz, x), h * 2 + c)
        greet(vid(h, zz, x), h * 2 + c)

        @pl.when(h != l)
        def _():
            greet(vid(h, zz, x), me_f)

    for dx in (2, 1, 3):

        @pl.when(h != l)
        def _():
            greet(vid(1 - h, z, xat(dx)), h * 2 + c)
            greet(vid(h, z, xat(dx)), h * 2 + c)

        greet(vid(1 - h, z, xat(dx)), me_f)
        greet(vid(h, z, xat(dx)), me_f)
    greet(vid(1 - h, z, x), h * 2 + c)
    greet(*lo_mate)
    greet(*core_mate)

    @pl.when(h != l)
    def _():
        greet(vid(1 - h, z, x), me_f)

    acc[...] = jnp.zeros_like(acc)
    own_copy.wait()

    @pl.when(h == l)
    def _():
        xg[p0] = mine[...]

    n_greet = 2 * (Z - 1) + 3 * (X - 1) + 3

    @pl.when(h == l)
    def _():
        pl.semaphore_wait(barrier, n_greet)

    @pl.when(h != l)
    def _():
        pl.semaphore_wait(barrier, n_greet + Z)


    def slot_copy(p, target):
        return pltpu.make_async_remote_copy(
            src_ref=xg.at[p],
            dst_ref=xg.at[p],
            send_sem=ssem.at[0],
            recv_sem=rsem.at[p],
            device_id=target,
            device_id_type=MESH,
        )

    def wait_slot(p):
        slot_copy(p, core_mate).wait_recv()

    def first_copy(zz, xx):
        return pltpu.make_async_remote_copy(
            src_ref=mine,
            dst_ref=xg.at[p0],
            send_sem=ssem.at[0],
            recv_sem=rsem.at[p0],
            device_id=(vid(l, zz, xx), h * 2 + c),
            device_id_type=MESH,
        )

    for dx in (2, 1, 3):
        first_copy(z, xat(dx)).start()
    first_copy(zat(offset(3)), x).start()
    first_copy(zat(offset(4)), x).start()
    first_copy(zat(offset(5)), x).start()
    first_copy(zat(offset(6)), x).start()

    @pl.when(h != l)
    def _():
        first_copy(z, x).start()

    def forward(p):
        s = l * n_half + p
        count = counts[s]
        block = xg[p]
        zero = jnp.zeros_like(block)
        right = []
        for k in range(SLOTS):
            ok = jnp.logical_and(k < count, cols[k, s] == c)
            r = rows[k, s]
            right.append(
                jnp.concatenate(
                    [
                        jnp.where(jnp.logical_and(ok, r == 0), block, zero),
                        jnp.where(jnp.logical_and(ok, r == 1), block, zero),
                    ],
                    axis=1,
                )
            )
        left = jnp.concatenate([tiles[p * SLOTS + k] for k in range(SLOTS)], axis=1)
        got = dot(left, jnp.concatenate(right, axis=0))
        acc[0] += got[:, :T]
        acc[1] += got[:, T:]

    def far_row(q):
        p = zat(offset(q)) * X + x
        wait_slot(p)
        for dx in (1, 3) if q < WIDE else (2, 1, 3):
            slot_copy(p, here(z, xat(dx))).start()

    def arrived(q, dx):
        p = zat(offset(q)) * X + xat(dx)
        wait_slot(p)
        forward(p)

    for dx in (1, 3, 2):
        p = z * X + xat(dx)
        wait_slot(p)
        if dx == 2:
            slot_copy(p, here(zat(2), x)).start()
            slot_copy(p, here(zat(-2), x)).start()
        slot_copy(p, here(zat(1), x)).start()
        slot_copy(p, here(zat(-1), x)).start()
    far_row(3)
    far_row(4)
    first_copy(zat(offset(7)), x).start()
    for copy in index_copies:
        copy.wait()
    tiles_copy.wait()

    @pl.when(h != l)
    def _():
        wait_slot(p0)

    forward(p0)
    far_row(5)
    far_row(6)
    first_copy(zat(offset(1)), x).start()
    first_copy(zat(offset(2)), x).start()
    forward(zat(offset(3)) * X + x)
    forward(zat(offset(4)) * X + x)
    far_row(7)
    forward(zat(offset(5)) * X + x)
    forward(zat(offset(6)) * X + x)
    forward(zat(offset(7)) * X + x)

    def this_row(dx, carry):
        forward(z * X + xat(dx))
        return carry

    lax.fori_loop(1, X, this_row, 0)
    arrived(1, 0)
    arrived(2, 0)

    def beside(t, carry):
        arrived(t // 3 + 1, t % 3 + 1)
        return carry

    lax.fori_loop(0, 6, beside, 0)

    def far(t, carry):
        arrived(NEAR + t // 3, t % 3 + 1)
        return carry

    lax.fori_loop(0, (Z - NEAR) * 3, far, 0)

    def exchange(src, dst, i, target):
        return pltpu.make_async_remote_copy(
            src_ref=src,
            dst_ref=dst,
            send_sem=exs.at[i],
            recv_sem=exr.at[i],
            device_id=target,
            device_id_type=MESH,
        )

    first = exchange(acc.at[1 - c], ex.at[0], 0, core_mate)
    first.start()
    first.wait_recv()
    sb[...] = acc[c] + ex[0]
    parts = [pl.ds(0, T // 2), pl.ds(T // 2, T // 2)]
    seconds = [exchange(sb.at[d], ex.at[1, d], 1 + 4 * i, lo_mate) for i, d in enumerate(parts)]
    thirds = [exchange(axf.at[c, d], axf.at[c, d], 2 + 4 * i, core_mate) for i, d in enumerate(parts)]
    for copy in seconds:
        copy.start()
    w_copy.wait()
    bias_copy.wait()
    cot_copy.wait()
    for d, second, third in zip(parts, seconds, thirds):
        second.wait_recv()
        axf[c, d] = sb[d] + ex[1, d]
        third.start()

    def rows_half(r):
        high, low = split(axf[r])
        pre = dot(high, w[...]) + dot(low, w[...]) + bias[...]
        result, slope = gelu_parts(pre)
        where = pl.ds(pl.multiple_of(r * T, T), T)
        out_ref[where, :] = result.astype(BF16)
        grad = (cot[where, :].astype(F32) * slope).astype(BF16)
        gp[r] = grad
        back = dot(w[...], grad, ((1,), (1,)))
        for cc in range(2):
            for ll in range(2):
                pt[cc, r, ll * 32 : ll * 32 + 32, :] = back[ll * 64 + cc * 32 : ll * 64 + cc * 32 + 32, :]

    rows_half(c)
    for i, d in enumerate(parts):
        exchange(axf.at[c, d], axf.at[1 - c, d], 2 + 4 * i, core_mate).wait_recv()
    rows_half(1 - c)

    p_first = exchange(pt.at[1 - c], pe.at[0], 3, core_mate)
    p_first.start()

    local_w = jnp.zeros((T, T), F32)
    local_b = jnp.zeros((1, T), F32)
    for r in range(2):
        high, low = split(axf[r])
        grad = gp[r]
        local_w += dot(high, grad, ((0,), (0,))) + dot(low, grad, ((0,), (0,)))
        local_b += jnp.sum(grad.astype(F32), axis=0, keepdims=True)
    spread_b = jnp.broadcast_to(local_b, (8, T))
    for i in range(E):
        gwb[i, :R, :] = local_w[i * R : i * R + R, :]
        gwb[i, R:, :] = spread_b

    me_e = h * X + x

    def e_at(i):
        hh = (h + i // X) % 2
        xx = xat(i % X)
        return hh * X + xx, (vid(hh, z, xx), me_f)

    def weight_copy(src, dst, send, recv, target):
        return pltpu.make_async_remote_copy(
            src_ref=src, dst_ref=dst, send_sem=send, recv_sem=recv, device_id=target, device_id_type=MESH
        )

    for i in range(1, E):
        e, target = e_at(i)
        weight_copy(gwb.at[e], g1.at[me_e], gsem.at[0], g1r.at[me_e], target).start()

    p_first.wait_recv()
    chip_p = pt[c] + pe[0]
    pb[...] = chip_p.astype(BF16)
    p_second = exchange(pb, pq, 4, lo_mate)
    p_second.start()
    p_second.wait_recv()
    pf[...] = (chip_p + pq[...].astype(F32)).astype(BF16)

    def own(p):
        s = l * n_half + p
        count = counts[s]
        low = pf[0]
        high = pf[1]
        zero = jnp.zeros_like(low)
        left = []
        for k in range(SLOTS):
            ok = k < count
            col = cols[k, s]
            picked = jnp.where(rows[k, s] == 0, low, high)
            left.append(
                jnp.concatenate(
                    [
                        jnp.where(jnp.logical_and(ok, col == 0), picked, zero),
                        jnp.where(jnp.logical_and(ok, col == 1), picked, zero),
                    ],
                    axis=0,
                )
            )
        right = tiles[pl.ds(p * SLOTS, SLOTS)].reshape(SLOTS * T, T)
        return dot(jnp.concatenate(left, axis=1), right)

    def sum_copy(i, target):
        return pltpu.make_async_remote_copy(
            src_ref=sbuf.at[i],
            dst_ref=rbuf.at[i],
            send_sem=tsem.at[0],
            recv_sem=trsem.at[i],
            device_id=target,
            device_id_type=MESH,
        )

    def take(i):
        sum_copy(i, core_mate).wait_recv()
        return rbuf[i].astype(F32)

    def put(i, value, target):
        sbuf[i] = value.astype(BF16)
        sum_copy(i, target).start()

    def weight_sums_one():
        total = gwb[me_e]
        for i in range(1, E):
            e, target = e_at(i)
            weight_copy(gwb.at[e], g1.at[e], gsem.at[0], g1r.at[e], target).wait_recv()
            total = total + g1[e]
        g2s[...] = total
        for dz in range(1, Z):
            weight_copy(g2s, g2.at[z], gsem.at[1], g2r.at[z], here(zat(dz), x)).start()

    def weight_sums_two():
        total = g2s[...]
        for dz in range(1, Z):
            zz = zat(dz)
            weight_copy(g2s, g2.at[zz], gsem.at[1], g2r.at[zz], here(zz, x)).wait_recv()
            total = total + g2[zz]
        g3[me_e] = total[:R, :]
        gb_ref[...] = total[R : R + 1, :]
        for i in range(1, E):
            e, target = e_at(i)
            weight_copy(g3.at[me_e], g3.at[me_e], gsem.at[2], g3r.at[me_e], target).start()

    def row_to(q):
        return zat(-offset(q))

    NS = Z + X - 1

    def final_copy(i, lp, slot, target):
        return pltpu.make_async_remote_copy(
            src_ref=fs.at[i, lp],
            dst_ref=fr.at[slot],
            send_sem=fsem.at[0],
            recv_sem=frsem.at[slot],
            device_id=target,
            device_id_type=MESH,
        )

    def deliver(value, i, zz, xx):
        value = value.astype(BF16)
        for lp in range(2):
            for ct in range(2):
                fs[i, lp, ct] = value[ct * 64 + lp * 32 : ct * 64 + lp * 32 + 32, :]
            is_self = jnp.logical_and(jnp.logical_and(h == l, l == lp), i == 0)

            @pl.when(jnp.logical_not(is_self))
            def _():
                final_copy(i, lp, h * NS + i, (vid(l, zz, xx), lp * 2 + c)).start()

            @pl.when(is_self)
            def _():
                fr[h * NS + i] = fs[i, lp]

    def x_put(zz, dx):
        put(zz * 3 + dx - 1, own(zz * X + xat(dx)), here(z, xat(dx)))

    def beside_z(q, dx):
        zz = row_to(q)
        put(3 * Z + (q - 1) * 3 + dx - 1, own(zz * X + xat(dx)), here(zz, x))

    def first_sums(t, carry):
        q = Z - 1 - t
        zz = row_to(q)

        @pl.when(q >= WIDE)
        def _():
            x_put(zz, 2)

        x_put(zz, 1)
        x_put(zz, 3)

        @pl.when(t < X)
        def _():
            q_two = jnp.where(t == 0, 3, 1)
            dx = jnp.where(t == 0, 2, t)
            beside_z(q_two, dx)
            beside_z(q_two + 1, dx)

        return carry

    lax.fori_loop(0, Z - NEAR, first_sums, 0)

    def same_column(q, carry):
        zz = row_to(q)
        deliver(own(zz * X + x), q, zz, x)
        return carry

    weight_sums_one()

    def this_row_x(dx):
        value = own(z * X + xat(dx)) + take(3 * Z + dx - 1) + take(3 * Z + 3 + dx - 1)
        if dx == 2:
            value = value + take(3 * Z + 6 + dx - 1) + take(3 * Z + 9 + dx - 1)
        deliver(value, Z - 1 + dx, z, xat(dx))


    def far_z(columns, t, carry):
        q = Z - 1 - t
        zz = row_to(q)
        value = own(zz * X + x)
        for dx in columns:
            value = value + take(zz * 3 + dx - 1)
        deliver(value, q, zz, x)
        return carry

    lax.fori_loop(0, Z - WIDE, functools.partial(far_z, (1, 3, 2)), 0)
    lax.fori_loop(Z - WIDE, Z - NEAR, functools.partial(far_z, (1, 3)), 0)
    for dx in (1, 3, 2):
        this_row_x(dx)
    lax.fori_loop(0, NEAR, same_column, 0)
    weight_sums_two()

    def arrive(slot, carry):
        is_self = jnp.logical_and(h == l, slot == h * NS)

        @pl.when(jnp.logical_not(is_self))
        def _():
            final_copy(0, 0, slot, core_mate).wait_recv()

        return carry

    lax.fori_loop(0, 2 * NS, arrive, 0)
    both = fr[0].astype(F32)
    for slot in range(1, 2 * NS):
        both = both + fr[slot].astype(F32)
    for ct in range(2):
        gf_ref[:, ct * T : ct * T + T] = both[ct].astype(BF16)

    for i in range(1, E):
        e, target = e_at(i)
        weight_copy(g3.at[e], g3.at[e], gsem.at[2], g3r.at[e], target).wait_recv()
    gw_ref[...] = g3[...].reshape(T, T)

    first.wait_send()
    for copy in seconds + thirds:
        copy.wait_send()
    p_first.wait_send()
    p_second.wait_send()
    n_sent = Z * X - 1

    def drained(ref, sem):
        pltpu.make_async_remote_copy(
            src_ref=ref,
            dst_ref=ref,
            send_sem=sem,
            recv_sem=rsem.at[0],
            device_id=core_mate,
            device_id_type=MESH,
        ).wait_send()

    drained(xg.at[pl.ds(0, n_sent)], ssem.at[0])
    drained(rbuf.at[pl.ds(0, 3 * (Z - NEAR) + 6)], tsem.at[0])
    drained(fr.at[pl.ds(0, 2 * NS - 1)], fsem.at[0])

    @pl.when(h != l)
    def _():
        drained(mine, ssem.at[0])
        drained(fr.at[0], fsem.at[0])

    drained(g1.at[pl.ds(0, E - 1)], gsem.at[0])
    drained(g2.at[pl.ds(0, Z - 1)], gsem.at[1])
    drained(g3.at[pl.ds(0, E - 1)], gsem.at[2])


def write_out(*refs):
    for source, target in zip(refs[:4], refs[4:]):
        target[...] = source[...]


def on_device(features, weight, bias, cotangent, adj_tiles, tile_rows, tile_cols, tile_counts):
    X = RING_X
    Z = lax.axis_size("vtx") // (2 * X)
    n_half = Z * X
    E = 2 * X
    R = T // E
    n_final = Z + X - 1
    anywhere = pl.BlockSpec(memory_space=pl.ANY)
    vmem = pl.BlockSpec(memory_space=pltpu.VMEM)
    n_buf = 3 * Z + 12
    out, gf, gw, gb = pl.pallas_call(
        functools.partial(kernel, Z),
        out_shape=(
            jax.ShapeDtypeStruct((2 * T, T), BF16),
            jax.ShapeDtypeStruct((32, 2 * T), BF16),
            jax.ShapeDtypeStruct((T, T), F32),
            jax.ShapeDtypeStruct((1, T), F32),
        ),
        in_specs=[anywhere] * 8,
        out_specs=(vmem, vmem, vmem, vmem),
        scratch_shapes=[
            pltpu.SMEM((SLOTS, 2 * n_half), jnp.int32),
            pltpu.SMEM((SLOTS, 2 * n_half), jnp.int32),
            pltpu.SMEM((2 * n_half,), jnp.int32),
            pltpu.VMEM((T, T), BF16),
            pltpu.VMEM((n_half, T, T), BF16),
            pltpu.VMEM((n_half * SLOTS, T, T), BF16),
            pltpu.VMEM((T, T), BF16),
            pltpu.VMEM((1, T), F32),
            pltpu.VMEM((2 * T, T), BF16),
            pltpu.VMEM((2, T, T), F32),
            pltpu.VMEM((2, T, T), F32),
            pltpu.VMEM((T, T), F32),
            pltpu.VMEM((2, T, T), F32),
            pltpu.VMEM((2, T, T), BF16),
            pltpu.VMEM((2, 2, 64, T), F32),
            pltpu.VMEM((1, 2, 64, T), F32),
            pltpu.VMEM((2, 64, T), BF16),
            pltpu.VMEM((2, 64, T), BF16),
            pltpu.VMEM((2, 64, T), BF16),
            pltpu.VMEM((E, R + 8, T), F32),
            pltpu.VMEM((E, R + 8, T), F32),
            pltpu.VMEM((R + 8, T), F32),
            pltpu.VMEM((Z, R + 8, T), F32),
            pltpu.VMEM((E, R, T), F32),
            pltpu.VMEM((n_buf, T, T), BF16),
            pltpu.VMEM((n_buf, T, T), BF16),
            pltpu.VMEM((n_final, 2, 2, 32, T), BF16),
            pltpu.VMEM((2 * n_final, 2, 32, T), BF16),
            pltpu.SemaphoreType.DMA((8,)),
            pltpu.SemaphoreType.DMA((1,)),
            pltpu.SemaphoreType.DMA((n_half,)),
            pltpu.SemaphoreType.DMA((7,)),
            pltpu.SemaphoreType.DMA((7,)),
            pltpu.SemaphoreType.DMA((3,)),
            pltpu.SemaphoreType.DMA((E,)),
            pltpu.SemaphoreType.DMA((Z,)),
            pltpu.SemaphoreType.DMA((E,)),
            pltpu.SemaphoreType.DMA((1,)),
            pltpu.SemaphoreType.DMA((n_buf,)),
            pltpu.SemaphoreType.DMA((1,)),
            pltpu.SemaphoreType.DMA((2 * n_final,)),
        ],
        compiler_params=pltpu.CompilerParams(
            collective_id=0, has_side_effects=True, vmem_limit_bytes=60 * 1024 * 1024
        ),
        cost_estimate=pl.CostEstimate(flops=2 * 10**9, bytes_accessed=5 * 10**6, transcendentals=32768),
    )(features, weight, bias.reshape(1, T), cotangent, adj_tiles, tile_rows.T, tile_cols.T, tile_counts)
    results = (out, gf, gw, gb)
    out, gf, gw, gb = pl.pallas_call(
        write_out,
        out_shape=tuple(jax.ShapeDtypeStruct(a.shape, a.dtype) for a in results),
        in_specs=[vmem] * 4,
        out_specs=(vmem,) * 4,
    )(*results)
    return out, gf.T, gw, gb.reshape(T)


def solution(mesh):
    in_specs = (
        P("vtx", None),
        P(None, "feat"),
        P("feat"),
        P("vtx", "feat"),
        P("vtx", None, None),
        P("vtx", None),
        P("vtx", None),
        P("vtx"),
    )
    out_specs = (P("vtx", "feat"), P("vtx", "feat"), P(None, "feat"), P("feat"))
    return jax.shard_map(on_device, mesh=mesh, in_specs=in_specs, out_specs=out_specs, check_vma=False)
```
